512 devices in a mesh: dp: 16 (over z), mp: 32 (over y, x, core).
Axes of the slice: x: 4, y: 4, z: 16, core: 2. Of those that a mesh axis runs over, the one named last changes fastest.
Arguments:
- normed_input: bfloat16 [16384, 5120], P(('dp', 'mp')), may hold values from -6 to 6
- key_gradient: bfloat16 [16384, 1024], P(('dp', 'mp')), may hold values from -6 to 6
- value_gradient: bfloat16 [16384, 1024], P(('dp', 'mp')), may hold values from -6 to 6
- frozen_key_weight: bfloat16 [5120, 1024], P('mp'), may hold values from -0.078125 to 0.078125
- frozen_value_weight: bfloat16 [5120, 1024], P('mp'), may hold values from -0.078125 to 0.078125
- key_down_weight: bfloat16 [64, 32, 5120], P(None, None, 'mp'), may hold values from -0.078125 to 0.078125
- value_down_weight: bfloat16 [64, 32, 5120], P(None, None, 'mp'), may hold values from -0.078125 to 0.078125
- key_up_weight: bfloat16 [64, 32, 1024], P(None, None, 'mp'), may hold values from -0.1875 to 0.1875
- value_up_weight: bfloat16 [64, 32, 1024], P(None, None, 'mp'), may hold values from -0.1875 to 0.1875
- tenant_of_block: int32 [16, 8], P('dp'), may hold values from 0 to 63, as said below
- live_token_count: int32 [16, 8], P('dp'), may hold values from 1 to 128, as said below
Outputs:
- grad_in: bfloat16 [16384, 5120], P(('dp', 'mp'))
- grad_a_key: float32 [64, 32, 5120], P('dp', None, 'mp')
- grad_a_value: float32 [64, 32, 5120], P('dp', None, 'mp')
- grad_b_key: float32 [64, 32, 1024], P('dp', None, 'mp')
- grad_b_value: float32 [64, 32, 1024], P('dp', None, 'mp')
The draws below stay inside these ranges and needn't reach their ends.
Inputs may be any that keep to these rules, and one draw needn't show every extreme that they name: `tenant_of_block`: each group's blocks form tenant segments: runs of blocks of one tenant. `live_token_count`: the live tokens of a block are its first ones; the rest is padding.
All inputs are finite; a program needn't handle non-finite values.
Results may differ from the reference program's by a relative error of at most 0.001.
Values may be sent and summed in bfloat16 or wider, within the bound.
No kernel may reach another device: no remote copies, remote signals or barrier semaphores. Data moves between devices by JAX's collectives and lax.ppermute only.
A program may use at most 64 MiB of HBM per device.

```python
import jax
import jax.numpy as jnp
from jax import lax

MODEL_WIDTH = 5120
KEY_VALUE_WIDTH = 1024
ADAPTER_RANK = 32
TENANT_COUNT = 64
BLOCK = 128
TOK_DEV = 32
BLOCKS = 8
TOKENS = 16384
N_DP = 16
N_MP = 32


def segment_starts(key):
    starts = jax.random.randint(jax.random.fold_in(key, 11), (N_DP, BLOCKS), 0, 2)
    first_column = jnp.arange(BLOCKS, dtype=jnp.int32)[None, :] == 0
    return jnp.where(first_column, 1, starts).astype(jnp.int32)


def draw_tenant_of_block(key, part):
    starts = segment_starts(key)
    key = jax.random.fold_in(key, 1)
    position = jnp.cumsum(starts, axis=1) - 1
    table = jax.random.randint(key, (N_DP, BLOCKS), 0, TENANT_COUNT)
    tenant_index = jnp.take_along_axis(table, position, axis=1)
    spot = jax.random.randint(jax.random.fold_in(key, 2), (), 0, N_DP * BLOCKS)
    flat = tenant_index.reshape(N_DP * BLOCKS)
    flat = jnp.where(jnp.arange(N_DP * BLOCKS, dtype=jnp.int32) == spot, TENANT_COUNT - 1, flat)
    return flat.reshape(N_DP, BLOCKS).astype(jnp.int32)


def draw_live_token_count(key, part):
    starts = segment_starts(key)
    key = jax.random.fold_in(key, 2)
    following = jnp.concatenate([starts[:, 1:], jnp.ones((N_DP, 1), jnp.int32)], axis=1)
    tails = jax.random.randint(key, (N_DP, BLOCKS), 1, BLOCK + 1)
    live = jnp.where(following == 1, tails, BLOCK)
    spot = jax.random.randint(jax.random.fold_in(key, 3), (), 0, N_DP * BLOCKS)
    flat = live.reshape(N_DP * BLOCKS)
    flat = jnp.where(jnp.arange(N_DP * BLOCKS, dtype=jnp.int32) == spot, BLOCK, flat)
    return flat.reshape(N_DP, BLOCKS).astype(jnp.int32)


def block_scale(key, shape, split, low, largest):
    gain = 1.0
    for axis_at, blocks in split:
        heights = jax.random.uniform(jax.random.fold_in(jax.random.fold_in(key, 6), axis_at), (blocks,), jnp.float32, low / len(split), largest / len(split))
        gain = gain * jnp.repeat(jnp.exp(heights), shape[axis_at] // blocks).reshape((-1,) + (1,) * (len(shape) - 1 - axis_at))
    return gain


def centred(stream_key, dims, scale, bound, pieces=(), kind=jnp.bfloat16):
    gain = block_scale(stream_key, dims, pieces, -0.22, 0.18) if pieces else 1.0
    array = jax.random.normal(stream_key, dims, jnp.float32) * scale * gain
    return jnp.minimum(jnp.maximum(array, -bound), bound).astype(kind)


def setup_inputs(seed: int = 0) -> dict:
    streams_of = jax.random.split(jax.random.key(seed), 12)
    return {
        "normed_input": centred(streams_of[0], (TOKENS, MODEL_WIDTH), 1.0, 6.0, ((0, 512),)),
        "key_gradient": centred(streams_of[1], (TOKENS, KEY_VALUE_WIDTH), 1.0, 6.0, ((0, 512),)),
        "value_gradient": centred(streams_of[2], (TOKENS, KEY_VALUE_WIDTH), 1.0, 6.0, ((0, 512),)),
        "frozen_key_weight": centred(streams_of[3], (MODEL_WIDTH, KEY_VALUE_WIDTH), MODEL_WIDTH ** -0.5, 0.078125, ((0, 32),)),
        "frozen_value_weight": centred(streams_of[4], (MODEL_WIDTH, KEY_VALUE_WIDTH), MODEL_WIDTH ** -0.5, 0.078125, ((0, 32),)),
        "key_down_weight": centred(streams_of[5], (TENANT_COUNT, ADAPTER_RANK, MODEL_WIDTH), MODEL_WIDTH ** -0.5, 0.078125, ((2, 32),)),
        "value_down_weight": centred(streams_of[6], (TENANT_COUNT, ADAPTER_RANK, MODEL_WIDTH), MODEL_WIDTH ** -0.5, 0.078125, ((2, 32),)),
        "key_up_weight": centred(streams_of[7], (TENANT_COUNT, ADAPTER_RANK, KEY_VALUE_WIDTH), KEY_VALUE_WIDTH ** -0.5, 0.1875, ((2, 32),)),
        "value_up_weight": centred(streams_of[8], (TENANT_COUNT, ADAPTER_RANK, KEY_VALUE_WIDTH), KEY_VALUE_WIDTH ** -0.5, 0.1875, ((2, 32),)),
        "tenant_of_block": draw_tenant_of_block(jax.random.fold_in(streams_of[11], 71), 0),
        "live_token_count": draw_live_token_count(jax.random.fold_in(streams_of[11], 71), 0),
    }


SCALE = 0.5


def reference(normed_input, key_gradient, value_gradient, frozen_key_weight, frozen_value_weight, key_down_weight, value_down_weight, key_up_weight, value_up_weight, tenant_of_block, live_token_count):
    single_float = jnp.float32
    high = lax.Precision.HIGHEST
    group_rows = TOK_DEV * N_MP
    blocks = group_rows // BLOCK
    hidden = normed_input.reshape(N_DP, group_rows, MODEL_WIDTH)
    cot_key = key_gradient.reshape(N_DP, group_rows, KEY_VALUE_WIDTH)
    cot_value = value_gradient.reshape(N_DP, group_rows, KEY_VALUE_WIDTH)

    def one_group(carry, inputs):
        inputs_x, key_in, value_in, tenant_index, live_counts = inputs
        offsets = jnp.arange(BLOCK, dtype=jnp.int32)
        live = (offsets[None, :] < live_counts[:, None]).astype(jnp.bfloat16).reshape(group_rows)
        masked_key = key_in * live[:, None]
        masked_value = value_in * live[:, None]
        x_blocks = inputs_x.reshape(blocks, BLOCK, MODEL_WIDTH).astype(single_float)
        key_blocks = masked_key.reshape(blocks, BLOCK, KEY_VALUE_WIDTH).astype(single_float)
        value_blocks = masked_value.reshape(blocks, BLOCK, KEY_VALUE_WIDTH).astype(single_float)
        chosen_key_down = key_down_weight[tenant_index].astype(single_float)
        chosen_value_down = value_down_weight[tenant_index].astype(single_float)
        chosen_key_up = key_up_weight[tenant_index].astype(single_float)
        chosen_value_up = value_up_weight[tenant_index].astype(single_float)
        down_key = jnp.einsum("brd,bsd->brs", chosen_key_down, x_blocks, precision=high)
        down_value = jnp.einsum("brd,bsd->brs", chosen_value_down, x_blocks, precision=high)
        back_key = jnp.einsum("brc,bsc->brs", chosen_key_up, key_blocks, precision=high)
        back_value = jnp.einsum("brc,bsc->brs", chosen_value_up, value_blocks, precision=high)
        base = jnp.dot(masked_key, frozen_key_weight.T, preferred_element_type=single_float) + jnp.dot(masked_value, frozen_value_weight.T, preferred_element_type=single_float)
        lowrank = jnp.einsum("brs,brd->bsd", back_key, chosen_key_down, precision=high) + jnp.einsum("brs,brd->bsd", back_value, chosen_value_down, precision=high)
        grad_rows = (base + SCALE * lowrank.reshape(group_rows, MODEL_WIDTH)).astype(jnp.bfloat16)
        onehot = (tenant_index[:, None] == jnp.arange(TENANT_COUNT, dtype=jnp.int32)[None, :]).astype(single_float)
        part_a_key = SCALE * jnp.einsum("brs,bsd->brd", back_key, x_blocks, precision=high)
        part_a_value = SCALE * jnp.einsum("brs,bsd->brd", back_value, x_blocks, precision=high)
        part_b_key = SCALE * jnp.einsum("brs,bsc->brc", down_key, key_blocks, precision=high)
        part_b_value = SCALE * jnp.einsum("brs,bsc->brc", down_value, value_blocks, precision=high)
        sums = (
            carry[0] + jnp.einsum("bt,brd->trd", onehot, part_a_key, precision=high),
            carry[1] + jnp.einsum("bt,brd->trd", onehot, part_a_value, precision=high),
            carry[2] + jnp.einsum("bt,brc->trc", onehot, part_b_key, precision=high),
            carry[3] + jnp.einsum("bt,brc->trc", onehot, part_b_value, precision=high),
        )
        return sums, grad_rows

    start = (
        jnp.zeros((TENANT_COUNT, ADAPTER_RANK, MODEL_WIDTH), single_float),
        jnp.zeros((TENANT_COUNT, ADAPTER_RANK, MODEL_WIDTH), single_float),
        jnp.zeros((TENANT_COUNT, ADAPTER_RANK, KEY_VALUE_WIDTH), single_float),
        jnp.zeros((TENANT_COUNT, ADAPTER_RANK, KEY_VALUE_WIDTH), single_float),
    )
    sums, grad_rows = lax.scan(one_group, start, (hidden, cot_key, cot_value, tenant_of_block, live_token_count))
    grad_in = grad_rows.reshape(N_DP * group_rows, MODEL_WIDTH)
    return grad_in, sums[0], sums[1], sums[2], sums[3]
```

```python
import functools

import jax
import jax.numpy as jnp
from jax import lax
from jax.experimental import pallas as pl
from jax.experimental.pallas import tpu as pltpu
from jax.sharding import Mesh, PartitionSpec as P

BLOCK = 128
SCALE = 0.5
F32 = jnp.float32
BF16 = jnp.bfloat16
VMEM = pl.BlockSpec(memory_space=pltpu.VMEM)
SMEM = pl.BlockSpec(memory_space=pltpu.SMEM)
ANY = pl.BlockSpec(memory_space=pl.ANY)
PARAMS = pltpu.CompilerParams(vmem_limit_bytes=24 * 1024 * 1024)
LANE = 128


def pack_kernel(
    tenants, counts, where, x_ref, k_ref, v_ref, up_ref, ak_hbm, av_hbm,
    send_ref, masked_ref, ak, av, sems,
):
    n_mp = send_ref.shape[0]
    blocks = ak.shape[0]
    rank = ak.shape[1]
    tok = x_ref.shape[0]
    feat = ak.shape[2]
    cols = k_ref.shape[1] // n_mp
    rest = feat - LANE
    quad = n_mp // blocks
    copies = []
    for b in range(blocks):
        t = tenants[0, b]
        copies.append(pltpu.make_async_copy(ak_hbm.at[t], ak.at[b], sems.at[0, b]))
        copies.append(pltpu.make_async_copy(av_hbm.at[t], av.at[b], sems.at[1, b]))
    for c in copies:
        c.start()
    me = where[0]
    count = counts[0, me // quad]
    row = lax.broadcasted_iota(jnp.int32, (tok, 1), 0) + (me % quad) * tok
    live = row < count
    mk = jnp.where(live, k_ref[...].astype(F32), 0.0).astype(BF16)
    mv = jnp.where(live, v_ref[...].astype(F32), 0.0).astype(BF16)
    masked_ref[:, : mk.shape[1]] = mk
    masked_ref[:, mk.shape[1] :] = mv
    x = x_ref[...]
    for j in range(n_mp):
        send_ref[j, 96:128, :] = x[:, feat * j : feat * j + LANE]
        last = x[:, feat * j + LANE : feat * (j + 1)]
        send_ref[j, 128:160, :] = jnp.concatenate(
            [last, mk[:, cols * j : cols * (j + 1)], last, mv[:, cols * j : cols * (j + 1)]], axis=1
        )
    for c in copies:
        c.wait()
    for b in range(blocks):
        a0 = ak[b]
        a1 = av[b]
        main = jnp.concatenate([a0[:, :LANE], a1[:, :LANE]], axis=0)
        up = up_ref[b]
        tail = jnp.concatenate(
            [a0[:, LANE:], up[:, :cols], a1[:, LANE:], up[:, cols : 2 * cols]], axis=1
        )
        for q in range(quad):
            send_ref[quad * b + q, 0:64, :] = main
            send_ref[quad * b + q, 64:96, :] = tail


def lane_mask(rows, slot):
    lane = lax.broadcasted_iota(jnp.int32, (rows, LANE), 1)
    return (lane >= 32 * slot) & (lane < 32 * slot + 32)


def vector_kernel(send_ref, recv_ref, out_ref):
    n_mp = send_ref.shape[0]
    masks = [lane_mask(32, s) for s in (0, 2, 1, 3)]
    total = jnp.zeros((32, LANE), F32)
    zero = jnp.zeros((64, LANE), BF16)
    for m in range(n_mp):
        lhs = jnp.concatenate([send_ref[m, 96:128, :], send_ref[m, 128:160, :]], axis=1)
        main = jnp.concatenate([recv_ref[m, 0:64, :], zero], axis=0)
        tail = recv_ref[m, 64:96, :]
        tails = jnp.concatenate([jnp.where(k, tail, jnp.zeros_like(tail)) for k in masks], axis=0)
        rhs = jnp.concatenate([main, tails], axis=1)
        total += lax.dot_general(lhs, rhs, (((1,), (1,)), ((), ())), preferred_element_type=F32)
    for m in range(n_mp):
        out_ref[m] = total


def split(x):
    hi = x.astype(BF16)
    return hi, (x - hi.astype(F32)).astype(BF16)


def parts_kernel(tenants, vec_ref, recv_ref, out_ref):
    blocks = vec_ref.shape[0] // 4
    out_ref[...] = jnp.zeros_like(out_ref)
    m0, m1, m2, m3 = [lane_mask(32, s) for s in range(4)]
    for b in range(blocks):
        vec = vec_ref[4 * b : 4 * b + 4].reshape(BLOCK, LANE) * SCALE
        lhs = jnp.concatenate(split(vec), axis=0)
        first = recv_ref[4 * b : 4 * b + 4, 96:128, :].reshape(BLOCK, LANE)
        second = recv_ref[4 * b : 4 * b + 4, 128:160, :].reshape(BLOCK, LANE)
        rhs = jnp.concatenate([first, second], axis=1)
        rhs = jnp.concatenate([rhs, rhs], axis=0)
        p = lax.dot_general(lhs, rhs, (((0,), (0,)), ((), ())), preferred_element_type=F32)
        t = tenants[0, b]
        out_ref[t, 0:64, :] += p[64:128, :LANE]
        q = p[:, LANE:]
        tail = jnp.where(m0, q[64:96], jnp.where(m1, q[0:32], jnp.where(m2, q[96:128], q[32:64])))
        out_ref[t, 64:96, :] += tail


def base_kernel(kv_ref, w_ref, vec_ref, a_ref, out_ref):
    blocks = a_ref.shape[0]
    per = kv_ref.shape[0] // blocks
    w = w_ref[...].reshape(-1, w_ref.shape[-1])
    for b in range(blocks):
        rows = kv_ref[per * b : per * (b + 1)].reshape(-1, kv_ref.shape[-1])
        vec = vec_ref[per * b : per * (b + 1)].reshape(-1, LANE)[:, 64:] * SCALE
        low = jnp.concatenate(split(vec), axis=1)
        a = a_ref[b].reshape(-1, LANE)
        dims = (((1,), (1,)), ((), ()))
        res = lax.dot_general(rows, w, dims, preferred_element_type=F32)
        res += lax.dot_general(low, a, dims, preferred_element_type=F32)
        out_ref[per * b : per * (b + 1)] = res.astype(BF16).reshape(per, -1, w.shape[0])


def finish_kernel(sum_ref, ak_ref, av_ref, bk_ref, bv_ref):
    for t in range(sum_ref.shape[0]):
        tail = sum_ref[t, 64:96, :]
        ak_ref[t, :, :LANE] = sum_ref[t, 0:32, :]
        ak_ref[t, :, LANE:] = tail[:, 0:32]
        av_ref[t, :, :LANE] = sum_ref[t, 32:64, :]
        av_ref[t, :, LANE:] = tail[:, 64:96]
        bk_ref[t] = tail[:, 32:64]
        bv_ref[t] = tail[:, 96:128]


def shards(x, kg, vg, wk, wv, ak, av, bk, bv, tenant_of_block, live_token_count):
    mp = ("y", "x", "core")
    n_mp = lax.axis_size(mp)
    tok, width = x.shape
    blocks = tenant_of_block.shape[1]
    feat = wk.shape[0]
    kv_width = kg.shape[1]
    tenants, rank = ak.shape[:2]
    me = lax.axis_index(mp).astype(jnp.int32).reshape(1)
    core = lax.axis_index("core")
    tenant_index = tenant_of_block[0]

    up = jnp.concatenate([bk[tenant_index], bv[tenant_index]], axis=-1)
    send, masked = pl.pallas_call(
        pack_kernel,
        out_shape=(
            jax.ShapeDtypeStruct((n_mp, 160, LANE), BF16),
            jax.ShapeDtypeStruct((tok, 2 * kv_width), BF16),
        ),
        in_specs=[SMEM, SMEM, SMEM, VMEM, VMEM, VMEM, VMEM, ANY, ANY],
        out_specs=(VMEM, VMEM),
        scratch_shapes=[
            pltpu.VMEM((blocks, rank, feat), BF16),
            pltpu.VMEM((blocks, rank, feat), BF16),
            pltpu.SemaphoreType.DMA((2, blocks)),
        ],
        compiler_params=PARAMS,
        name="pack",
    )(tenant_of_block, live_token_count, me, x, kg, vg, up, ak, av)
    recv = lax.all_to_all(send, mp, split_axis=0, concat_axis=0, tiled=True)
    vec_send = pl.pallas_call(
        vector_kernel,
        out_shape=jax.ShapeDtypeStruct((n_mp, tok, LANE), F32),
        in_specs=[VMEM, VMEM],
        out_specs=VMEM,
        compiler_params=PARAMS,
        name="vectors",
    )(send, recv)
    vec = lax.all_to_all(vec_send, mp, split_axis=0, concat_axis=0, tiled=True)
    parts = pl.pallas_call(
        parts_kernel,
        out_shape=jax.ShapeDtypeStruct((tenants, 96, LANE), F32),
        in_specs=[SMEM, VMEM, VMEM],
        out_specs=VMEM,
        compiler_params=PARAMS,
        name="parts",
    )(tenant_of_block, vec, recv)
    parts, masked, wk, wv = lax.optimization_barrier((parts, masked, wk, wv))
    sums = lax.psum_scatter(parts, "dp", scatter_dimension=0, tiled=True)

    def spread(a, axes):
        n = lax.axis_size(axes)
        return lax.all_to_all(
            jnp.broadcast_to(a[None], (n, *a.shape)), axes, split_axis=0, concat_axis=0, tiled=True
        )

    chosen = jnp.concatenate([ak[tenant_index], av[tenant_index]], axis=1)
    chosen = jnp.concatenate([chosen, chosen], axis=1).transpose(0, 2, 1)
    kv = spread(masked, ("y", "x"))
    w = spread(jnp.concatenate([wk, wv], axis=1), ("core",))
    a = spread(chosen, ("core",)).transpose(1, 0, 2, 3)
    mine = lax.dynamic_index_in_dim(vec.reshape(n_mp // 2, 2, tok, LANE), core, 1, keepdims=False)
    grad = pl.pallas_call(
        base_kernel,
        out_shape=jax.ShapeDtypeStruct((n_mp // 2, tok, 2 * feat), BF16),
        in_specs=[VMEM, VMEM, VMEM, VMEM],
        out_specs=VMEM,
        compiler_params=PARAMS,
        name="base",
    )(kv, w, mine, a)
    grad = lax.all_to_all(grad, ("y", "x"), split_axis=0, concat_axis=0, tiled=True)
    grad_in = grad.transpose(1, 0, 2).reshape(tok, width)

    owned = tenants // lax.axis_size("dp")
    grads = pl.pallas_call(
        finish_kernel,
        out_shape=(
            jax.ShapeDtypeStruct((owned, rank, feat), F32),
            jax.ShapeDtypeStruct((owned, rank, feat), F32),
            jax.ShapeDtypeStruct((owned, rank, bk.shape[2]), F32),
            jax.ShapeDtypeStruct((owned, rank, bk.shape[2]), F32),
        ),
        in_specs=[VMEM],
        out_specs=(VMEM, VMEM, VMEM, VMEM),
        compiler_params=PARAMS,
        name="finish",
    )(sums)
    return (grad_in, *grads)


def solution(mesh):
    n_dp, n_mp = mesh.devices.shape
    fine = Mesh(mesh.devices.reshape(n_dp, 4, n_mp // 8, 2), ("dp", "y", "x", "core"))
    mp = ("y", "x", "core")
    rows = P(("dp", *mp), None)
    in_specs = (
        rows, rows, rows,
        P(mp, None), P(mp, None),
        P(None, None, mp), P(None, None, mp), P(None, None, mp), P(None, None, mp),
        P("dp", None), P("dp", None),
    )
    grads = P("dp", None, mp)
    return jax.shard_map(
        shards, mesh=fine, in_specs=in_specs, out_specs=(rows, grads, grads, grads, grads),
        check_vma=False,
    )
```

```python
import functools

import jax
import jax.numpy as jnp
from jax import lax
from jax.experimental import pallas as pl
from jax.experimental.pallas import tpu as pltpu
from jax.sharding import Mesh, PartitionSpec as P

BLOCK = 128
SCALE = 0.5
F32 = jnp.float32
BF16 = jnp.bfloat16
VMEM = pl.BlockSpec(memory_space=pltpu.VMEM)
SMEM = pl.BlockSpec(memory_space=pltpu.SMEM)
ANY = pl.BlockSpec(memory_space=pl.ANY)
PARAMS = pltpu.CompilerParams(vmem_limit_bytes=24 * 1024 * 1024)
LANE = 128


def pack_kernel(
    tenants, counts, where, x_ref, k_ref, v_ref, bk_ref, bv_ref, ak_hbm, av_hbm,
    send_ref, masked_ref, empty_hbm, ak, av, up, zeros, sems, zero_sems,
):
    n_mp = send_ref.shape[0]
    blocks = ak.shape[0]
    rank = ak.shape[1]
    tok = x_ref.shape[0]
    feat = ak.shape[2]
    cols = k_ref.shape[1] // n_mp
    rest = feat - LANE
    quad = n_mp // blocks
    copies = []
    for b in range(blocks):
        t = tenants[0, b]
        copies.append(pltpu.make_async_copy(ak_hbm.at[t], ak.at[b], sems.at[0, b]))
        copies.append(pltpu.make_async_copy(av_hbm.at[t], av.at[b], sems.at[1, b]))
    for c in copies:
        c.start()
    zeros[...] = jnp.zeros_like(zeros)
    chunk = zeros.shape[0]
    fills = [
        pltpu.make_async_copy(zeros, empty_hbm.at[pl.ds(i * chunk, chunk)], zero_sems.at[i])
        for i in range(empty_hbm.shape[0] // chunk)
    ]
    for c in fills:
        c.start()
    me = where[0]
    count = counts[0, me // quad]
    row = lax.broadcasted_iota(jnp.int32, (tok, 1), 0) + (me % quad) * tok
    live = row < count
    mk = jnp.where(live, k_ref[...].astype(F32), 0.0).astype(BF16)
    mv = jnp.where(live, v_ref[...].astype(F32), 0.0).astype(BF16)
    masked_ref[:, : mk.shape[1]] = mk
    masked_ref[:, mk.shape[1] :] = mv
    x = x_ref[...]
    for j in range(n_mp):
        send_ref[j, 96:128, :] = x[:, feat * j : feat * j + LANE]
        last = x[:, feat * j + LANE : feat * (j + 1)]
        send_ref[j, 128:160, :] = jnp.concatenate(
            [last, mk[:, cols * j : cols * (j + 1)], last, mv[:, cols * j : cols * (j + 1)]], axis=1
        )
    which = lax.broadcasted_iota(jnp.int32, (blocks, bk_ref.shape[2]), 0)
    tenant = jnp.zeros_like(which)
    for b in range(blocks):
        tenant = jnp.where(which == b, tenants[0, b], tenant)
    hot = lax.broadcasted_iota(jnp.int32, tenant.shape, 1) == tenant
    hot = jnp.where(hot, 1.0, 0.0).astype(BF16)
    for ref, at in ((bk_ref, 32), (bv_ref, 96)):
        flat = ref[...].reshape(rank * cols, ref.shape[2])
        got = lax.dot_general(hot, flat, (((1,), (1,)), ((), ())), preferred_element_type=F32)
        for r in range(rank):
            up[:, r, at : at + cols] = got[:, cols * r : cols * (r + 1)]
    for c in copies:
        c.wait()
    for b in range(blocks):
        a0 = ak[b]
        a1 = av[b]
        main = jnp.concatenate([a0[:, :LANE], a1[:, :LANE]], axis=0)
        near = up[b].astype(BF16)
        tail = jnp.concatenate(
            [a0[:, LANE:], near[:, 32:64], a1[:, LANE:], near[:, 96:128]], axis=1
        )
        for q in range(quad):
            send_ref[quad * b + q, 0:64, :] = main
            send_ref[quad * b + q, 64:96, :] = tail
    for c in fills:
        c.wait()


def lane_mask(rows, slot):
    lane = lax.broadcasted_iota(jnp.int32, (rows, LANE), 1)
    return (lane >= 32 * slot) & (lane < 32 * slot + 32)


def vector_kernel(send_ref, recv_ref, out_ref):
    n_mp = send_ref.shape[0]
    masks = [lane_mask(32, s) for s in (0, 2, 1, 3)]
    total = jnp.zeros((32, LANE), F32)
    zero = jnp.zeros((64, LANE), BF16)
    for m in range(n_mp):
        lhs = jnp.concatenate([send_ref[m, 96:128, :], send_ref[m, 128:160, :]], axis=1)
        main = jnp.concatenate([recv_ref[m, 0:64, :], zero], axis=0)
        tail = recv_ref[m, 64:96, :]
        tails = jnp.concatenate([jnp.where(k, tail, jnp.zeros_like(tail)) for k in masks], axis=0)
        rhs = jnp.concatenate([main, tails], axis=1)
        total += lax.dot_general(lhs, rhs, (((1,), (1,)), ((), ())), preferred_element_type=F32)
    for m in range(n_mp):
        out_ref[m] = total


def split(x):
    hi = x.astype(BF16)
    return hi, (x - hi.astype(F32)).astype(BF16)


def parts_kernel(tenants, vec_ref, recv_ref, empty_hbm, out_hbm, acc, sems):
    blocks = vec_ref.shape[0] // 4
    m0, m1, m2, m3 = [lane_mask(32, s) for s in range(4)]
    first = []
    for b in range(blocks):
        f = jnp.int32(b)
        for c in range(b - 1, -1, -1):
            f = jnp.where(tenants[0, c] == tenants[0, b], c, f)
        first.append(f)
    acc[...] = jnp.zeros_like(acc)
    for b in range(blocks):
        vec = vec_ref[4 * b : 4 * b + 4].reshape(BLOCK, LANE) * SCALE
        lhs = jnp.concatenate(split(vec), axis=0)
        near = recv_ref[4 * b : 4 * b + 4, 96:128, :].reshape(BLOCK, LANE)
        far = recv_ref[4 * b : 4 * b + 4, 128:160, :].reshape(BLOCK, LANE)
        rhs = jnp.concatenate([near, far], axis=1)
        rhs = jnp.concatenate([rhs, rhs], axis=0)
        p = lax.dot_general(lhs, rhs, (((0,), (0,)), ((), ())), preferred_element_type=F32)
        q = p[:, LANE:]
        tail = jnp.where(m0, q[64:96], jnp.where(m1, q[0:32], jnp.where(m2, q[96:128], q[32:64])))
        acc[first[b], 0:64, :] += p[64:128, :LANE]
        acc[first[b], 64:96, :] += tail
    copies = [
        pltpu.make_async_copy(acc.at[b], out_hbm.at[tenants[0, b]], sems.at[b])
        for b in range(blocks)
    ]
    for b in range(blocks):
        pl.when(first[b] == b)(copies[b].start)
    for b in range(blocks):
        pl.when(first[b] == b)(copies[b].wait)


def base_kernel(kv_ref, w_ref, vec_ref, a_ref, out_ref):
    blocks = a_ref.shape[0]
    per = kv_ref.shape[0] // blocks
    w = w_ref[...].reshape(-1, w_ref.shape[-1])
    for b in range(blocks):
        rows = kv_ref[per * b : per * (b + 1)].reshape(-1, kv_ref.shape[-1])
        vec = vec_ref[per * b : per * (b + 1)].reshape(-1, LANE)[:, 64:] * SCALE
        low = jnp.concatenate(split(vec), axis=1)
        a = a_ref[b].reshape(-1, LANE)
        dims = (((1,), (1,)), ((), ()))
        res = lax.dot_general(rows, w, dims, preferred_element_type=F32)
        res += lax.dot_general(low, a, dims, preferred_element_type=F32)
        out_ref[per * b : per * (b + 1)] = res.astype(BF16).reshape(per, -1, w.shape[0])


def finish_kernel(sum_ref, ak_ref, av_ref, bk_ref, bv_ref):
    for t in range(sum_ref.shape[0]):
        tail = sum_ref[t, 64:96, :]
        ak_ref[t, :, :LANE] = sum_ref[t, 0:32, :]
        ak_ref[t, :, LANE:] = tail[:, 0:32]
        av_ref[t, :, :LANE] = sum_ref[t, 32:64, :]
        av_ref[t, :, LANE:] = tail[:, 64:96]
        bk_ref[t] = tail[:, 32:64]
        bv_ref[t] = tail[:, 96:128]


def shards(x, kg, vg, wk, wv, ak, av, bk, bv, tenant_of_block, live_token_count):
    mp = ("y", "x", "core")
    n_mp = lax.axis_size(mp)
    tok, width = x.shape
    blocks = tenant_of_block.shape[1]
    feat = wk.shape[0]
    kv_width = kg.shape[1]
    tenants, rank = ak.shape[:2]
    me = lax.axis_index(mp).astype(jnp.int32).reshape(1)
    core = lax.axis_index("core")
    tenant_index = tenant_of_block[0]

    packed = (tenants, 96, LANE)
    send, masked, empty = pl.pallas_call(
        pack_kernel,
        out_shape=(
            jax.ShapeDtypeStruct((n_mp, 160, LANE), BF16),
            jax.ShapeDtypeStruct((tok, 2 * kv_width), BF16),
            jax.ShapeDtypeStruct(packed, F32),
        ),
        in_specs=[SMEM, SMEM, SMEM, VMEM, VMEM, VMEM, VMEM, VMEM, ANY, ANY],
        out_specs=(VMEM, VMEM, ANY),
        scratch_shapes=[
            pltpu.VMEM((blocks, rank, feat), BF16),
            pltpu.VMEM((blocks, rank, feat), BF16),
            pltpu.VMEM((blocks, rank, LANE), F32),
            pltpu.VMEM((tenants // 8, 96, LANE), F32),
            pltpu.SemaphoreType.DMA((2, blocks)),
            pltpu.SemaphoreType.DMA((8,)),
        ],
        compiler_params=PARAMS,
        name="pack",
    )(
        tenant_of_block, live_token_count, me, x, kg, vg,
        bk.transpose(1, 2, 0), bv.transpose(1, 2, 0), ak, av,
    )
    recv = lax.all_to_all(send, mp, split_axis=0, concat_axis=0, tiled=True)
    vec_send = pl.pallas_call(
        vector_kernel,
        out_shape=jax.ShapeDtypeStruct((n_mp, tok, LANE), F32),
        in_specs=[VMEM, VMEM],
        out_specs=VMEM,
        compiler_params=PARAMS,
        name="vectors",
    )(send, recv)
    vec = lax.all_to_all(vec_send, mp, split_axis=0, concat_axis=0, tiled=True)
    parts = pl.pallas_call(
        parts_kernel,
        out_shape=jax.ShapeDtypeStruct(packed, F32),
        in_specs=[SMEM, VMEM, VMEM, ANY],
        out_specs=ANY,
        scratch_shapes=[
            pltpu.VMEM((blocks, 96, LANE), F32),
            pltpu.SemaphoreType.DMA((blocks,)),
        ],
        input_output_aliases={3: 0},
        compiler_params=PARAMS,
        name="parts",
    )(tenant_of_block, vec, recv, empty)
    parts, masked, wk, wv = lax.optimization_barrier((parts, masked, wk, wv))
    sums = lax.psum_scatter(parts, "dp", scatter_dimension=0, tiled=True)

    def spread(a, axes):
        n = lax.axis_size(axes)
        return lax.all_to_all(
            jnp.broadcast_to(a[None], (n, *a.shape)), axes, split_axis=0, concat_axis=0, tiled=True
        )

    chosen = jnp.concatenate([ak[tenant_index], av[tenant_index]], axis=1)
    chosen = jnp.concatenate([chosen, chosen], axis=1).transpose(0, 2, 1)
    kv = spread(masked, ("y", "x"))
    w = spread(jnp.concatenate([wk, wv], axis=1), ("core",))
    a = spread(chosen, ("core",)).transpose(1, 0, 2, 3)
    mine = lax.dynamic_index_in_dim(vec.reshape(n_mp // 2, 2, tok, LANE), core, 1, keepdims=False)
    grad = pl.pallas_call(
        base_kernel,
        out_shape=jax.ShapeDtypeStruct((n_mp // 2, tok, 2 * feat), BF16),
        in_specs=[VMEM, VMEM, VMEM, VMEM],
        out_specs=VMEM,
        compiler_params=PARAMS,
        name="base",
    )(kv, w, mine, a)
    grad = lax.all_to_all(grad, ("y", "x"), split_axis=0, concat_axis=0, tiled=True)
    grad_in = grad.transpose(1, 0, 2).reshape(tok, width)

    owned = tenants // lax.axis_size("dp")
    grads = pl.pallas_call(
        finish_kernel,
        out_shape=(
            jax.ShapeDtypeStruct((owned, rank, feat), F32),
            jax.ShapeDtypeStruct((owned, rank, feat), F32),
            jax.ShapeDtypeStruct((owned, rank, bk.shape[2]), F32),
            jax.ShapeDtypeStruct((owned, rank, bk.shape[2]), F32),
        ),
        in_specs=[VMEM],
        out_specs=(VMEM, VMEM, VMEM, VMEM),
        compiler_params=PARAMS,
        name="finish",
    )(sums)
    return (grad_in, *grads)


def solution(mesh):
    n_dp, n_mp = mesh.devices.shape
    fine = Mesh(mesh.devices.reshape(n_dp, 4, n_mp // 8, 2), ("dp", "y", "x", "core"))
    mp = ("y", "x", "core")
    rows = P(("dp", *mp), None)
    in_specs = (
        rows, rows, rows,
        P(mp, None), P(mp, None),
        P(None, None, mp), P(None, None, mp), P(None, None, mp), P(None, None, mp),
        P("dp", None), P("dp", None),
    )
    grads = P("dp", None, mp)
    return jax.shard_map(
        shards, mesh=fine, in_specs=in_specs, out_specs=(rows, grads, grads, grads, grads),
        check_vma=False,
    )
```

```python
import functools

import jax
import jax.numpy as jnp
from jax import lax
from jax.experimental import pallas as pl
from jax.experimental.pallas import tpu as pltpu
from jax.sharding import Mesh, PartitionSpec as P

BLOCK = 128
SCALE = 0.5
F32 = jnp.float32
BF16 = jnp.bfloat16
VMEM = pl.BlockSpec(memory_space=pltpu.VMEM)
SMEM = pl.BlockSpec(memory_space=pltpu.SMEM)
HBM = pl.BlockSpec(memory_space=pltpu.HBM)
PARAMS = pltpu.CompilerParams(vmem_limit_bytes=24 * 1024 * 1024)
LANE = 128


FILLS = (6, 10, 16)


def start_fills(zeros, out_hbm, sems, first, last):
    zeros[...] = jnp.zeros_like(zeros)
    chunk = out_hbm.shape[0] // FILLS[-1]
    fills = [
        pltpu.make_async_copy(zeros, out_hbm.at[pl.ds(i * chunk, chunk)], sems.at[i - first])
        for i in range(first, last)
    ]
    for c in fills:
        c.start()
    return fills


def pack_kernel(
    where, tenants_hbm, counts_hbm, x_hbm, k_hbm, v_hbm, bk_hbm, bv_hbm, ak_hbm, av_hbm,
    send_ref, masked_ref, chosen_ref, empty_hbm,
    tenants, counts, x_ref, k_ref, v_ref, bk_ref, bv_ref, ak, av, up, zeros, sems, a_sems, fill_sems,
):
    n_mp = send_ref.shape[0]
    blocks, rank, feat = ak.shape
    tok, kv_width = k_ref.shape
    cols = kv_width // n_mp
    quad = n_mp // blocks
    pairs = (
        (tenants_hbm, tenants), (counts_hbm, counts), (x_hbm, x_ref), (k_hbm, k_ref),
        (v_hbm, v_ref), (bk_hbm, bk_ref), (bv_hbm, bv_ref),
    )
    loads = [pltpu.make_async_copy(src, dst, sems.at[i]) for i, (src, dst) in enumerate(pairs)]
    for c in loads:
        c.start()
    fills = start_fills(zeros, empty_hbm, fill_sems, 0, FILLS[0])
    loads[0].wait()
    copies = []
    for b in range(blocks):
        t = tenants[0, b]
        copies.append(pltpu.make_async_copy(ak_hbm.at[t], ak.at[b], a_sems.at[0, b]))
        copies.append(pltpu.make_async_copy(av_hbm.at[t], av.at[b], a_sems.at[1, b]))
    for c in copies:
        c.start()
    for c in loads[1:]:
        c.wait()
    me = where[0]
    count = counts[0, me // quad]
    row = lax.broadcasted_iota(jnp.int32, (tok, 1), 0) + (me % quad) * tok
    live = row < count
    mk = jnp.where(live, k_ref[...].astype(F32), 0.0).astype(BF16)
    mv = jnp.where(live, v_ref[...].astype(F32), 0.0).astype(BF16)
    masked_ref[:, :kv_width] = mk
    masked_ref[:, kv_width:] = mv
    x = x_ref[...]
    for j in range(n_mp):
        send_ref[j, 96:128, :] = x[:, feat * j : feat * j + LANE]
        last = x[:, feat * j + LANE : feat * (j + 1)]
        send_ref[j, 128:160, :] = jnp.concatenate(
            [last, mk[:, cols * j : cols * (j + 1)], last, mv[:, cols * j : cols * (j + 1)]], axis=1
        )
    which = lax.broadcasted_iota(jnp.int32, (blocks, bk_ref.shape[2]), 0)
    tenant = jnp.zeros_like(which)
    for b in range(blocks):
        tenant = jnp.where(which == b, tenants[0, b], tenant)
    hot = lax.broadcasted_iota(jnp.int32, tenant.shape, 1) == tenant
    hot = jnp.where(hot, 1.0, 0.0).astype(BF16)
    for ref, at in ((bk_ref, 32), (bv_ref, 96)):
        flat = ref[...].reshape(rank * cols, ref.shape[2])
        got = lax.dot_general(hot, flat, (((1,), (1,)), ((), ())), preferred_element_type=F32)
        for r in range(rank):
            up[:, r, at : at + cols] = got[:, cols * r : cols * (r + 1)]
    for c in copies:
        c.wait()
    for b in range(blocks):
        a0 = ak[b]
        a1 = av[b]
        main = jnp.concatenate([a0[:, :LANE], a1[:, :LANE]], axis=0)
        near = up[b].astype(BF16)
        tail = jnp.concatenate(
            [a0[:, LANE:], near[:, 32:64], a1[:, LANE:], near[:, 96:128]], axis=1
        )
        for q in range(quad):
            send_ref[quad * b + q, 0:64, :] = main
            send_ref[quad * b + q, 64:96, :] = tail
        for c in range(2):
            chosen_ref[c, b, :rank, :] = a0
            chosen_ref[c, b, rank:, :] = a1
    for c in fills:
        c.wait()


def lane_mask(rows, slot):
    lane = lax.broadcasted_iota(jnp.int32, (rows, LANE), 1)
    return (lane >= 32 * slot) & (lane < 32 * slot + 32)


def vector_kernel(send_ref, recv_ref, empty_hbm, out_ref, more_hbm, zeros, fill_sems):
    n_mp = send_ref.shape[0]
    fills = start_fills(zeros, more_hbm, fill_sems, FILLS[0], FILLS[1])
    masks = [lane_mask(32, s) for s in (0, 2, 1, 3)]
    total = jnp.zeros((32, LANE), F32)
    zero = jnp.zeros((64, LANE), BF16)
    for m in range(n_mp):
        lhs = jnp.concatenate([send_ref[m, 96:128, :], send_ref[m, 128:160, :]], axis=1)
        main = jnp.concatenate([recv_ref[m, 0:64, :], zero], axis=0)
        tail = recv_ref[m, 64:96, :]
        tails = jnp.concatenate([jnp.where(k, tail, jnp.zeros_like(tail)) for k in masks], axis=0)
        rhs = jnp.concatenate([main, tails], axis=1)
        total += lax.dot_general(lhs, rhs, (((1,), (1,)), ((), ())), preferred_element_type=F32)
    for m in range(n_mp):
        out_ref[m] = total
    for c in fills:
        c.wait()


def split(x):
    hi = x.astype(BF16)
    return hi, (x - hi.astype(F32)).astype(BF16)


def parts_kernel(
    where, tenants, vec_ref, recv_ref, more_hbm, out_hbm, low_ref, acc, zeros, sems, fill_sems
):
    blocks = vec_ref.shape[0] // 4
    fills = start_fills(zeros, out_hbm, fill_sems, FILLS[1], FILLS[2])
    m0, m1, m2, m3 = [lane_mask(32, s) for s in range(4)]
    first = []
    for b in range(blocks):
        f = jnp.int32(b)
        for c in range(b - 1, -1, -1):
            f = jnp.where(tenants[0, c] == tenants[0, b], c, f)
        first.append(f)
    acc[...] = jnp.zeros_like(acc)
    for b in range(blocks):
        vec = vec_ref[4 * b : 4 * b + 4].reshape(BLOCK, LANE) * SCALE
        lhs = jnp.concatenate(split(vec), axis=0)
        near = recv_ref[4 * b : 4 * b + 4, 96:128, :].reshape(BLOCK, LANE)
        far = recv_ref[4 * b : 4 * b + 4, 128:160, :].reshape(BLOCK, LANE)
        rhs = jnp.concatenate([near, far], axis=1)
        rhs = jnp.concatenate([rhs, rhs], axis=0)
        p = lax.dot_general(lhs, rhs, (((0,), (0,)), ((), ())), preferred_element_type=F32)
        q = p[:, LANE:]
        tail = jnp.where(m0, q[64:96], jnp.where(m1, q[0:32], jnp.where(m2, q[96:128], q[32:64])))
        acc[first[b], 0:64, :] += p[64:128, :LANE]
        acc[first[b], 64:96, :] += tail
    for c in fills:
        c.wait()
    copies = [
        pltpu.make_async_copy(acc.at[b], out_hbm.at[tenants[0, b]], sems.at[b])
        for b in range(blocks)
    ]
    for b in range(blocks):
        pl.when(first[b] == b)(copies[b].start)
    core = where[0] % 2
    for i in range(low_ref.shape[0]):
        back = vec_ref[2 * i + core][:, 64:] * SCALE
        low_ref[i] = jnp.concatenate(split(back), axis=1)
    for b in range(blocks):
        pl.when(first[b] == b)(copies[b].wait)


def base_kernel(kv_ref, w_ref, low_ref, a_ref, out_ref):
    blocks = a_ref.shape[1]
    per = kv_ref.shape[0] // blocks
    w = w_ref[...].reshape(-1, w_ref.shape[-1])
    for b in range(blocks):
        rows = kv_ref[per * b : per * (b + 1)].reshape(-1, kv_ref.shape[-1])
        low = low_ref[per * b : per * (b + 1)].reshape(-1, LANE)
        res = lax.dot_general(rows, w, (((1,), (1,)), ((), ())), preferred_element_type=F32)
        add = []
        for c in range(2):
            a = a_ref[c, b]
            a = jnp.concatenate([a, a], axis=0)
            add.append(jnp.dot(low, a, preferred_element_type=F32))
        res += jnp.concatenate(add, axis=1)
        out_ref[per * b : per * (b + 1)] = res.astype(BF16).reshape(per, -1, w.shape[0])


def finish_kernel(sum_hbm, ak_ref, av_ref, bk_ref, bv_ref, sum_ref, sem):
    load = pltpu.make_async_copy(sum_hbm, sum_ref, sem)
    load.start()
    load.wait()
    for t in range(sum_ref.shape[0]):
        tail = sum_ref[t, 64:96, :]
        ak_ref[t, :, :LANE] = sum_ref[t, 0:32, :]
        ak_ref[t, :, LANE:] = tail[:, 0:32]
        av_ref[t, :, :LANE] = sum_ref[t, 32:64, :]
        av_ref[t, :, LANE:] = tail[:, 64:96]
        bk_ref[t] = tail[:, 32:64]
        bv_ref[t] = tail[:, 96:128]


def shards(x, kg, vg, wk, wv, ak, av, bk, bv, tenant_of_block, live_token_count):
    mp = ("y", "x", "core")
    n_mp = lax.axis_size(mp)
    tok, width = x.shape
    blocks = tenant_of_block.shape[1]
    feat = wk.shape[0]
    kv_width = kg.shape[1]
    tenants, rank = ak.shape[:2]
    me = lax.axis_index(mp).astype(jnp.int32).reshape(1)
    cols = bk.shape[2]
    hbm = lambda a: pltpu.with_memory_space_constraint(a, pltpu.HBM)
    packed = (tenants, 96, LANE)
    zeros = pltpu.VMEM((tenants // FILLS[-1], 96, LANE), F32)
    send, masked, chosen, empty = pl.pallas_call(
        pack_kernel,
        out_shape=(
            jax.ShapeDtypeStruct((n_mp, 160, LANE), BF16),
            jax.ShapeDtypeStruct((tok, 2 * kv_width), BF16),
            jax.ShapeDtypeStruct((2, blocks, 2 * rank, feat), BF16),
            jax.ShapeDtypeStruct(packed, F32),
        ),
        in_specs=[SMEM] + [HBM] * 9,
        out_specs=(VMEM, VMEM, VMEM, HBM),
        scratch_shapes=[
            pltpu.SMEM((1, blocks), jnp.int32),
            pltpu.SMEM((1, blocks), jnp.int32),
            pltpu.VMEM((tok, width), BF16),
            pltpu.VMEM((tok, kv_width), BF16),
            pltpu.VMEM((tok, kv_width), BF16),
            pltpu.VMEM((rank, cols, tenants), BF16),
            pltpu.VMEM((rank, cols, tenants), BF16),
            pltpu.VMEM((blocks, rank, feat), BF16),
            pltpu.VMEM((blocks, rank, feat), BF16),
            pltpu.VMEM((blocks, rank, LANE), F32),
            zeros,
            pltpu.SemaphoreType.DMA((7,)),
            pltpu.SemaphoreType.DMA((2, blocks)),
            pltpu.SemaphoreType.DMA((FILLS[0],)),
        ],
        compiler_params=PARAMS,
        name="pack",
    )(
        me, hbm(tenant_of_block), hbm(live_token_count), hbm(x), hbm(kg), hbm(vg),
        hbm(bk.transpose(1, 2, 0)), hbm(bv.transpose(1, 2, 0)), hbm(ak), hbm(av),
    )
    recv = lax.all_to_all(send, mp, split_axis=0, concat_axis=0, tiled=True)
    vec_send, empty = pl.pallas_call(
        vector_kernel,
        out_shape=(
            jax.ShapeDtypeStruct((n_mp, tok, LANE), F32),
            jax.ShapeDtypeStruct(packed, F32),
        ),
        in_specs=[VMEM, VMEM, HBM],
        out_specs=(VMEM, HBM),
        scratch_shapes=[zeros, pltpu.SemaphoreType.DMA((FILLS[1] - FILLS[0],))],
        input_output_aliases={2: 1},
        compiler_params=PARAMS,
        name="vectors",
    )(send, recv, empty)
    vec = lax.all_to_all(vec_send, mp, split_axis=0, concat_axis=0, tiled=True)
    parts, low = pl.pallas_call(
        parts_kernel,
        out_shape=(
            jax.ShapeDtypeStruct(packed, F32),
            jax.ShapeDtypeStruct((n_mp // 2, tok, LANE), BF16),
        ),
        in_specs=[SMEM, SMEM, VMEM, VMEM, HBM],
        out_specs=(HBM, VMEM),
        scratch_shapes=[
            pltpu.VMEM((blocks, 96, LANE), F32),
            zeros,
            pltpu.SemaphoreType.DMA((blocks,)),
            pltpu.SemaphoreType.DMA((FILLS[2] - FILLS[1],)),
        ],
        input_output_aliases={4: 0},
        compiler_params=PARAMS,
        name="parts",
    )(me, tenant_of_block, vec, recv, empty)
    parts, masked = lax.optimization_barrier((parts, masked))
    sums = lax.psum_scatter(parts, "dp", scatter_dimension=0, tiled=True)

    def swap(a, axes):
        return lax.all_to_all(a, axes, split_axis=0, concat_axis=0, tiled=True)

    a = swap(chosen, ("core",))
    both = jnp.concatenate([wk, wv], axis=1)
    w = swap(jnp.broadcast_to(both[None], (2, *both.shape)), ("core",))
    kv = swap(jnp.broadcast_to(masked[None], (n_mp // 2, *masked.shape)), ("y", "x"))
    grad = pl.pallas_call(
        base_kernel,
        out_shape=jax.ShapeDtypeStruct((n_mp // 2, tok, 2 * feat), BF16),
        in_specs=[VMEM, VMEM, VMEM, VMEM],
        out_specs=VMEM,
        compiler_params=PARAMS,
        name="base",
    )(kv, w, low, a)
    grad = swap(grad, ("y", "x"))
    grad_in = grad.transpose(1, 0, 2).reshape(tok, width)

    owned = tenants // lax.axis_size("dp")
    grads = pl.pallas_call(
        finish_kernel,
        out_shape=(
            jax.ShapeDtypeStruct((owned, rank, feat), F32),
            jax.ShapeDtypeStruct((owned, rank, feat), F32),
            jax.ShapeDtypeStruct((owned, rank, bk.shape[2]), F32),
            jax.ShapeDtypeStruct((owned, rank, bk.shape[2]), F32),
        ),
        in_specs=[HBM],
        out_specs=(VMEM, VMEM, VMEM, VMEM),
        scratch_shapes=[pltpu.VMEM((owned, 96, LANE), F32), pltpu.SemaphoreType.DMA],
        compiler_params=PARAMS,
        name="finish",
    )(hbm(sums))
    return (grad_in, *grads)


def solution(mesh):
    n_dp, n_mp = mesh.devices.shape
    fine = Mesh(mesh.devices.reshape(n_dp, 4, n_mp // 8, 2), ("dp", "y", "x", "core"))
    mp = ("y", "x", "core")
    rows = P(("dp", *mp), None)
    in_specs = (
        rows, rows, rows,
        P(mp, None), P(mp, None),
        P(None, None, mp), P(None, None, mp), P(None, None, mp), P(None, None, mp),
        P("dp", None), P("dp", None),
    )
    grads = P("dp", None, mp)
    return jax.shard_map(
        shards, mesh=fine, in_specs=in_specs, out_specs=(rows, grads, grads, grads, grads),
        check_vma=False,
    )
```

```python
import functools

import jax
import jax.numpy as jnp
from jax import lax
from jax.experimental import pallas as pl
from jax.experimental.pallas import tpu as pltpu
from jax.sharding import Mesh, PartitionSpec as P

BLOCK = 128
SCALE = 0.5
F32 = jnp.float32
BF16 = jnp.bfloat16
VMEM = pl.BlockSpec(memory_space=pltpu.VMEM)
SMEM = pl.BlockSpec(memory_space=pltpu.SMEM)
HBM = pl.BlockSpec(memory_space=pltpu.HBM)
PARAMS = pltpu.CompilerParams(vmem_limit_bytes=24 * 1024 * 1024)
LANE = 128


def pack_kernel(
    where, tenants_hbm, counts_hbm, x_hbm, k_hbm, v_hbm, bk_hbm, bv_hbm, ak_hbm, av_hbm, wk_hbm, wv_hbm,
    send_ref, masked_hbm, bundle_hbm,
    tenants, counts, x_ref, k_ref, v_ref, bk_ref, bv_ref, ak, av, up, masked, low, sems, a_sems, out_sems,
):
    n_mp = send_ref.shape[0]
    blocks, rank, feat = ak.shape
    tok, kv_width = k_ref.shape
    cols = kv_width // n_mp
    quad = n_mp // blocks
    pairs = (
        (tenants_hbm, tenants), (counts_hbm, counts), (x_hbm, x_ref), (k_hbm, k_ref),
        (v_hbm, v_ref), (bk_hbm, bk_ref), (bv_hbm, bv_ref),
    )
    loads = [pltpu.make_async_copy(src, dst, sems.at[i]) for i, (src, dst) in enumerate(pairs)]
    for c in loads:
        c.start()
    feat_rows = pl.ds(0, feat), pl.ds(feat, feat)
    stores = [
        pltpu.make_async_copy(wk_hbm, bundle_hbm.at[feat_rows[0]], out_sems.at[0]),
        pltpu.make_async_copy(wv_hbm, bundle_hbm.at[feat_rows[1]], out_sems.at[1]),
        pltpu.make_async_copy(masked, masked_hbm, out_sems.at[2]),
        pltpu.make_async_copy(low, bundle_hbm.at[pl.ds(2 * feat, low.shape[0])], out_sems.at[3]),
    ]
    stores[0].start()
    stores[1].start()
    loads[0].wait()
    copies = []
    for b in range(blocks):
        t = tenants[0, b]
        copies.append(pltpu.make_async_copy(ak_hbm.at[t], ak.at[b], a_sems.at[0, b]))
        copies.append(pltpu.make_async_copy(av_hbm.at[t], av.at[b], a_sems.at[1, b]))
    for c in copies:
        c.start()
    for c in loads[1:]:
        c.wait()
    me = where[0]
    count = counts[0, me // quad]
    row = lax.broadcasted_iota(jnp.int32, (tok, 1), 0) + (me % quad) * tok
    live = row < count
    mk = jnp.where(live, k_ref[...].astype(F32), 0.0).astype(BF16)
    mv = jnp.where(live, v_ref[...].astype(F32), 0.0).astype(BF16)
    masked[:, :kv_width] = mk
    masked[:, kv_width:] = mv
    stores[2].start()
    x = x_ref[...]
    for j in range(n_mp):
        send_ref[j, 96:128, :] = x[:, feat * j : feat * j + LANE]
        last = x[:, feat * j + LANE : feat * (j + 1)]
        send_ref[j, 128:160, :] = jnp.concatenate(
            [last, mk[:, cols * j : cols * (j + 1)], last, mv[:, cols * j : cols * (j + 1)]], axis=1
        )
    which = lax.broadcasted_iota(jnp.int32, (blocks, bk_ref.shape[2]), 0)
    tenant = jnp.zeros_like(which)
    for b in range(blocks):
        tenant = jnp.where(which == b, tenants[0, b], tenant)
    hot = lax.broadcasted_iota(jnp.int32, tenant.shape, 1) == tenant
    hot = jnp.where(hot, 1.0, 0.0).astype(BF16)
    for ref, at in ((bk_ref, 32), (bv_ref, 96)):
        flat = ref[...].reshape(rank * cols, ref.shape[2])
        got = lax.dot_general(hot, flat, (((1,), (1,)), ((), ())), preferred_element_type=F32)
        for r in range(rank):
            up[:, r, at : at + cols] = got[:, cols * r : cols * (r + 1)]
    for c in copies:
        c.wait()
    for b in range(blocks):
        at = slice(LANE * b, LANE * (b + 1))
        for i, ref in enumerate((ak, av)):
            low[rank * i : rank * (i + 1), at] = ref[b][:, :LANE]
            low[rank * (2 + i) : rank * (3 + i), LANE * b : LANE * b + feat - LANE] = ref[b][:, LANE:]
    stores[3].start()
    for b in range(blocks):
        a0 = ak[b]
        a1 = av[b]
        main = jnp.concatenate([a0[:, :LANE], a1[:, :LANE]], axis=0)
        near = up[b].astype(BF16)
        tail = jnp.concatenate(
            [a0[:, LANE:], near[:, 32:64], a1[:, LANE:], near[:, 96:128]], axis=1
        )
        for q in range(quad):
            send_ref[quad * b + q, 0:64, :] = main
            send_ref[quad * b + q, 64:96, :] = tail
    for c in stores:
        c.wait()


def lane_mask(rows, slot):
    lane = lax.broadcasted_iota(jnp.int32, (rows, LANE), 1)
    return (lane >= 32 * slot) & (lane < 32 * slot + 32)


def vector_kernel(send_ref, recv_ref, out_ref):
    n_mp = send_ref.shape[0]
    masks = [lane_mask(32, s) for s in (0, 2, 1, 3)]
    total = jnp.zeros((32, LANE), F32)
    zero = jnp.zeros((64, LANE), BF16)
    for m in range(n_mp):
        lhs = jnp.concatenate([send_ref[m, 96:128, :], send_ref[m, 128:160, :]], axis=1)
        main = jnp.concatenate([recv_ref[m, 0:64, :], zero], axis=0)
        tail = recv_ref[m, 64:96, :]
        tails = jnp.concatenate([jnp.where(k, tail, jnp.zeros_like(tail)) for k in masks], axis=0)
        rhs = jnp.concatenate([main, tails], axis=1)
        total += lax.dot_general(lhs, rhs, (((1,), (1,)), ((), ())), preferred_element_type=F32)
    for m in range(n_mp):
        out_ref[m] = total


def split(x):
    hi = x.astype(BF16)
    return hi, (x - hi.astype(F32)).astype(BF16)


def first_blocks(tenants, blocks):
    first = []
    for b in range(blocks):
        f = jnp.int32(b)
        for c in range(b - 1, -1, -1):
            f = jnp.where(tenants[0, c] == tenants[0, b], c, f)
        first.append(f)
    return first


PART = 96
HALF = 48


def parts_kernel(where, tenants, vec_ref, recv_ref, top_ref, bottom_ref, low_ref):
    blocks = vec_ref.shape[0] // 4
    m0, m1, m2, m3 = [lane_mask(32, s) for s in range(4)]
    first = first_blocks(tenants, blocks)
    top_ref[...] = jnp.zeros_like(top_ref)
    bottom_ref[...] = jnp.zeros_like(bottom_ref)
    for b in range(blocks):
        vec = vec_ref[4 * b : 4 * b + 4].reshape(BLOCK, LANE) * SCALE
        lhs = jnp.concatenate(split(vec), axis=0)
        near = recv_ref[4 * b : 4 * b + 4, 96:128, :].reshape(BLOCK, LANE)
        far = recv_ref[4 * b : 4 * b + 4, 128:160, :].reshape(BLOCK, LANE)
        rhs = jnp.concatenate([near, far], axis=1)
        rhs = jnp.concatenate([rhs, rhs], axis=0)
        p = lax.dot_general(lhs, rhs, (((0,), (0,)), ((), ())), preferred_element_type=F32)
        q = p[:, LANE:]
        tail = jnp.where(m0, q[64:96], jnp.where(m1, q[0:32], jnp.where(m2, q[96:128], q[32:64])))
        at = pl.multiple_of(first[b] * HALF, 8)
        top_ref[pl.ds(at, HALF), :] += p[64:112, :LANE]
        bottom_ref[pl.ds(at, HALF), :] += jnp.concatenate([p[112:128, :LANE], tail], axis=0)
    row = lax.broadcasted_iota(jnp.int32, (blocks, LANE), 0)
    ids = jnp.full((blocks, LANE), -1, jnp.int32)
    for b in range(blocks):
        ids = jnp.where((row == b) & (first[b] == b), tenants[0, b], ids)
    top_ref[blocks * HALF :, :] = ids.astype(F32)
    bottom_ref[blocks * HALF :, :] = ids.astype(F32)
    core = where[0] % 2
    for i in range(low_ref.shape[0]):
        back = vec_ref[2 * i + core][:, 64:] * SCALE
        low_ref[i] = jnp.concatenate(split(back), axis=1)


def kept(tenant, parity):
    return (tenant >= 0) & ((tenant // 4) % 2 == parity), (tenant // 8) * 4 + tenant % 4


def half_of(out_hbm, mine, place, h):
    return out_hbm.at[jnp.where(mine, place, 0), pl.ds(h * HALF, HALF)]


def own_kernel(plane, tenants, top_ref, bottom_ref, out_hbm, zeros, fill_sems, sems):
    blocks = sems.shape[1]
    zeros[...] = jnp.zeros_like(zeros)
    chunk = zeros.shape[0]
    fills = [
        pltpu.make_async_copy(zeros, out_hbm.at[pl.ds(i * chunk, chunk)], fill_sems.at[i])
        for i in range(out_hbm.shape[0] // chunk)
    ]
    for c in fills:
        c.start()
    first = first_blocks(tenants, blocks)
    for c in fills:
        c.wait()
    todo = []
    for b in range(blocks):
        mine, place = kept(tenants[0, b], plane[0] % 2)
        mine = mine & (first[b] == b)
        for h, ref in enumerate((top_ref, bottom_ref)):
            src = ref.at[pl.ds(b * HALF, HALF)]
            dst = half_of(out_hbm, mine, place, h)
            todo.append((mine, pltpu.make_async_copy(src, dst, sems.at[h, b])))
    for mine, copy in todo:
        pl.when(mine)(copy.start)
    for mine, copy in todo:
        pl.when(mine)(copy.wait)


def merge_kernel(plane, tenants, top_ref, bottom_ref, got_top, got_bottom, own_hbm, out_hbm, buf, sems):
    blocks = sems.shape[1]
    todo = []
    for h, (ref, got) in enumerate(((top_ref, got_top), (bottom_ref, got_bottom))):
        for b in range(blocks):
            tenant = jnp.max(got[blocks * HALF + b : blocks * HALF + b + 1, :]).astype(jnp.int32)
            mine, place = kept(tenant, plane[0] % 2)
            same = jnp.int32(-1)
            for c in range(blocks - 1, -1, -1):
                same = jnp.where(tenants[0, c] == tenant, c, same)
            at = pl.multiple_of(jnp.maximum(same, 0) * HALF, 8)
            here = jnp.where(same >= 0, 1.0, 0.0)
            buf[h, b] = got[b * HALF : (b + 1) * HALF, :] + ref[pl.ds(at, HALF), :] * here
            copy = pltpu.make_async_copy(buf.at[h, b], half_of(out_hbm, mine, place, h), sems.at[h, b])
            pl.when(mine)(copy.start)
            todo.append((mine, copy))
    for mine, copy in todo:
        pl.when(mine)(copy.wait)


def base_kernel(where, kv_ref, near_ref, far_ref, low_ref, out_ref, w):
    width = near_ref.shape[1]
    blocks = width // LANE
    feat = out_ref.shape[2] // 2
    per = kv_ref.shape[0] // blocks
    rank = (near_ref.shape[0] - 2 * feat) // 4
    core = where[0] % 2
    for c, ref in enumerate((near_ref, far_ref)):
        at = pl.multiple_of(jnp.where(core == 0, c, 1 - c) * feat, 16)
        w[pl.ds(at, feat), :width] = ref[0:feat, :]
        w[pl.ds(at, feat), width:] = ref[feat : 2 * feat, :]
    step = 4
    for s in range(0, blocks, step):
        rows = kv_ref[per * s : per * (s + step)].reshape(-1, kv_ref.shape[-1])
        res = lax.dot_general(rows, w[...], (((1,), (1,)), ((), ())), preferred_element_type=F32)
        size = res.shape[0] // step
        for i in range(step):
            b = s + i
            low = low_ref[per * b : per * (b + 1)].reshape(-1, LANE)
            add = []
            for ref in (near_ref, far_ref):
                main = ref[2 * feat : 2 * feat + 2 * rank, LANE * b : LANE * (b + 1)]
                rest = ref[2 * feat + 2 * rank :, LANE * b : LANE * b + feat - LANE]
                a = jnp.concatenate([main, rest], axis=1)
                add.append(jnp.dot(low, jnp.concatenate([a, a], axis=0), preferred_element_type=F32))
            swapped = jnp.concatenate(add[::-1], axis=1)
            add = jnp.where(core == 0, jnp.concatenate(add, axis=1), swapped)
            total = res[size * i : size * (i + 1)] + add
            out_ref[per * b : per * (b + 1)] = total.astype(BF16).reshape(per, -1, 2 * feat)


def finish_kernel(sum_hbm, ak_ref, av_ref, bk_ref, bv_ref, sum_ref, sem):
    load = pltpu.make_async_copy(sum_hbm, sum_ref, sem)
    load.start()
    load.wait()
    for t in range(sum_ref.shape[0]):
        tail = sum_ref[t, 64:96, :]
        ak_ref[t, :, :LANE] = sum_ref[t, 0:32, :]
        ak_ref[t, :, LANE:] = tail[:, 0:32]
        av_ref[t, :, :LANE] = sum_ref[t, 32:64, :]
        av_ref[t, :, LANE:] = tail[:, 64:96]
        bk_ref[t] = tail[:, 32:64]
        bv_ref[t] = tail[:, 96:128]


def shards(x, kg, vg, wk, wv, ak, av, bk, bv, tenant_of_block, live_token_count):
    mp = ("y", "x", "core")
    n_mp = lax.axis_size(mp)
    tok, width = x.shape
    blocks = tenant_of_block.shape[1]
    feat = wk.shape[0]
    kv_width = kg.shape[1]
    tenants, rank = ak.shape[:2]
    me = lax.axis_index(mp).astype(jnp.int32).reshape(1)
    cols = bk.shape[2]
    hbm = lambda a: pltpu.with_memory_space_constraint(a, pltpu.HBM)
    bundle_rows = 2 * feat + 4 * rank
    send, masked, bundle = pl.pallas_call(
        pack_kernel,
        out_shape=(
            jax.ShapeDtypeStruct((n_mp, 160, LANE), BF16),
            jax.ShapeDtypeStruct((tok, 2 * kv_width), BF16),
            jax.ShapeDtypeStruct((bundle_rows, kv_width), BF16),
        ),
        in_specs=[SMEM] + [HBM] * 11,
        out_specs=(VMEM, HBM, HBM),
        scratch_shapes=[
            pltpu.SMEM((1, blocks), jnp.int32),
            pltpu.SMEM((1, blocks), jnp.int32),
            pltpu.VMEM((tok, width), BF16),
            pltpu.VMEM((tok, kv_width), BF16),
            pltpu.VMEM((tok, kv_width), BF16),
            pltpu.VMEM((rank, cols, tenants), BF16),
            pltpu.VMEM((rank, cols, tenants), BF16),
            pltpu.VMEM((blocks, rank, feat), BF16),
            pltpu.VMEM((blocks, rank, feat), BF16),
            pltpu.VMEM((blocks, rank, LANE), F32),
            pltpu.VMEM((tok, 2 * kv_width), BF16),
            pltpu.VMEM((4 * rank, kv_width), BF16),
            pltpu.SemaphoreType.DMA((7,)),
            pltpu.SemaphoreType.DMA((2, blocks)),
            pltpu.SemaphoreType.DMA((4,)),
        ],
        compiler_params=PARAMS,
        name="pack",
    )(
        me, hbm(tenant_of_block), hbm(live_token_count), hbm(x), hbm(kg), hbm(vg),
        hbm(bk.transpose(1, 2, 0)), hbm(bv.transpose(1, 2, 0)), hbm(ak), hbm(av), hbm(wk), hbm(wv),
    )
    recv = lax.all_to_all(send, mp, split_axis=0, concat_axis=0, tiled=True)
    vec_send = pl.pallas_call(
        vector_kernel,
        out_shape=jax.ShapeDtypeStruct((n_mp, tok, LANE), F32),
        in_specs=[VMEM, VMEM],
        out_specs=VMEM,
        compiler_params=PARAMS,
        name="vectors",
    )(send, recv)
    vec = lax.all_to_all(vec_send, mp, split_axis=0, concat_axis=0, tiled=True)
    group = jax.ShapeDtypeStruct((blocks * HALF + blocks, LANE), F32)
    top, bottom, low = pl.pallas_call(
        parts_kernel,
        out_shape=(group, group, jax.ShapeDtypeStruct((n_mp // 2, tok, LANE), BF16)),
        in_specs=[SMEM, SMEM, VMEM, VMEM],
        out_specs=(VMEM, VMEM, VMEM),
        compiler_params=PARAMS,
        name="parts",
    )(me, tenant_of_block, vec, recv)

    dp = ("zh", "zl")
    n_dp = lax.axis_size(dp)
    pairs = [(z, z ^ 1) for z in range(n_dp)]
    others = [(z, (z + (1 if z % 2 else -1)) % n_dp) for z in range(n_dp)]
    got_top = lax.ppermute(top, dp, pairs)
    got_bottom = lax.ppermute(bottom, dp, others)
    plane = lax.axis_index("zl").astype(jnp.int32).reshape(1)
    half = jax.ShapeDtypeStruct((tenants // 2, PART, LANE), F32)
    own = pl.pallas_call(
        own_kernel,
        out_shape=half,
        in_specs=[SMEM, SMEM, VMEM, VMEM],
        out_specs=HBM,
        scratch_shapes=[
            pltpu.VMEM((tenants // 16, PART, LANE), F32),
            pltpu.SemaphoreType.DMA((8,)),
            pltpu.SemaphoreType.DMA((2, blocks)),
        ],
        compiler_params=PARAMS,
        name="own",
    )(plane, tenant_of_block, top, bottom)
    got_top, bundle = lax.optimization_barrier((got_top, bundle))
    far = lax.ppermute(bundle, "core", [(0, 1), (1, 0)])
    sums = pl.pallas_call(
        merge_kernel,
        out_shape=half,
        in_specs=[SMEM, SMEM, VMEM, VMEM, VMEM, VMEM, HBM],
        out_specs=HBM,
        scratch_shapes=[
            pltpu.VMEM((2, blocks, HALF, LANE), F32),
            pltpu.SemaphoreType.DMA((2, blocks)),
        ],
        input_output_aliases={6: 0},
        compiler_params=PARAMS,
        name="merge",
    )(plane, tenant_of_block, top, bottom, got_top, got_bottom, own)

    sums, masked = lax.optimization_barrier((sums, masked))
    sums = lax.psum_scatter(sums, "zh", scatter_dimension=0, tiled=True)

    def swap(a, axes):
        return lax.all_to_all(a, axes, split_axis=0, concat_axis=0, tiled=True)

    kv = swap(jnp.broadcast_to(masked[None], (n_mp // 2, *masked.shape)), ("y", "x"))
    grad = pl.pallas_call(
        base_kernel,
        out_shape=jax.ShapeDtypeStruct((n_mp // 2, tok, 2 * feat), BF16),
        in_specs=[SMEM] + [VMEM] * 4,
        out_specs=VMEM,
        scratch_shapes=[pltpu.VMEM((2 * feat, 2 * kv_width), BF16)],
        compiler_params=PARAMS,
        name="base",
    )(me, kv, bundle, far, low)
    grad = swap(grad, ("y", "x"))
    grad_in = grad.transpose(1, 0, 2).reshape(tok, width)
    sums, grad_in = lax.optimization_barrier((sums, grad_in))

    owned = tenants // lax.axis_size(("zh", "zl"))
    grads = pl.pallas_call(
        finish_kernel,
        out_shape=(
            jax.ShapeDtypeStruct((owned, rank, feat), F32),
            jax.ShapeDtypeStruct((owned, rank, feat), F32),
            jax.ShapeDtypeStruct((owned, rank, bk.shape[2]), F32),
            jax.ShapeDtypeStruct((owned, rank, bk.shape[2]), F32),
        ),
        in_specs=[HBM],
        out_specs=(VMEM, VMEM, VMEM, VMEM),
        scratch_shapes=[pltpu.VMEM((owned, PART, LANE), F32), pltpu.SemaphoreType.DMA],
        compiler_params=PARAMS,
        name="finish",
    )(hbm(sums))
    return (grad_in, *grads)


def solution(mesh):
    n_dp, n_mp = mesh.devices.shape
    fine = Mesh(
        mesh.devices.reshape(n_dp // 2, 2, 4, n_mp // 8, 2), ("zh", "zl", "y", "x", "core")
    )
    dp, mp = ("zh", "zl"), ("y", "x", "core")
    rows = P((*dp, *mp), None)
    in_specs = (
        rows, rows, rows,
        P(mp, None), P(mp, None),
        P(None, None, mp), P(None, None, mp), P(None, None, mp), P(None, None, mp),
        P(dp, None), P(dp, None),
    )
    grads = P(dp, None, mp)
    return jax.shard_map(
        shards, mesh=fine, in_specs=in_specs, out_specs=(rows, grads, grads, grads, grads),
        check_vma=False,
    )
```

```python
import functools

import jax
import jax.numpy as jnp
from jax import lax
from jax.experimental import pallas as pl
from jax.experimental.pallas import tpu as pltpu
from jax.sharding import Mesh, PartitionSpec as P

BLOCK = 128
SCALE = 0.5
F32 = jnp.float32
BF16 = jnp.bfloat16
VMEM = pl.BlockSpec(memory_space=pltpu.VMEM)
SMEM = pl.BlockSpec(memory_space=pltpu.SMEM)
HBM = pl.BlockSpec(memory_space=pltpu.HBM)
PARAMS = pltpu.CompilerParams(vmem_limit_bytes=24 * 1024 * 1024)
LANE = 128


def pack_kernel(
    where, tenants_hbm, counts_hbm, x_hbm, k_hbm, v_hbm, bk_hbm, bv_hbm, ak_hbm, av_hbm, wk_hbm, wv_hbm,
    send_ref, masked_hbm, bundle_hbm,
    tenants, counts, x_ref, k_ref, v_ref, bk_ref, bv_ref, ak, av, up, masked, low, sems, a_sems, out_sems,
):
    n_mp = send_ref.shape[0]
    blocks, rank, feat = ak.shape
    tok, kv_width = k_ref.shape
    cols = kv_width // n_mp
    quad = n_mp // blocks
    pairs = (
        (tenants_hbm, tenants), (counts_hbm, counts), (x_hbm, x_ref), (k_hbm, k_ref),
        (v_hbm, v_ref), (bk_hbm, bk_ref), (bv_hbm, bv_ref),
    )
    loads = [pltpu.make_async_copy(src, dst, sems.at[i]) for i, (src, dst) in enumerate(pairs)]
    for c in loads:
        c.start()
    feat_rows = pl.ds(0, feat), pl.ds(feat, feat)
    stores = [
        pltpu.make_async_copy(wk_hbm, bundle_hbm.at[feat_rows[0]], out_sems.at[0]),
        pltpu.make_async_copy(wv_hbm, bundle_hbm.at[feat_rows[1]], out_sems.at[1]),
        pltpu.make_async_copy(masked, masked_hbm, out_sems.at[2]),
        pltpu.make_async_copy(low, bundle_hbm.at[pl.ds(2 * feat, low.shape[0])], out_sems.at[3]),
    ]
    stores[0].start()
    stores[1].start()
    loads[0].wait()
    copies = []
    for b in range(blocks):
        t = tenants[0, b]
        copies.append(pltpu.make_async_copy(ak_hbm.at[t], ak.at[b], a_sems.at[0, b]))
        copies.append(pltpu.make_async_copy(av_hbm.at[t], av.at[b], a_sems.at[1, b]))
    for c in copies:
        c.start()
    for c in loads[1:]:
        c.wait()
    me = where[0]
    count = counts[0, me // quad]
    row = lax.broadcasted_iota(jnp.int32, (tok, 1), 0) + (me % quad) * tok
    live = row < count
    mk = jnp.where(live, k_ref[...].astype(F32), 0.0).astype(BF16)
    mv = jnp.where(live, v_ref[...].astype(F32), 0.0).astype(BF16)
    masked[:, :kv_width] = mk
    masked[:, kv_width:] = mv
    stores[2].start()
    x = x_ref[...]
    for j in range(n_mp):
        send_ref[j, 96:128, :] = x[:, feat * j : feat * j + LANE]
        last = x[:, feat * j + LANE : feat * (j + 1)]
        send_ref[j, 128:160, :] = jnp.concatenate(
            [last, mk[:, cols * j : cols * (j + 1)], last, mv[:, cols * j : cols * (j + 1)]], axis=1
        )
    which = lax.broadcasted_iota(jnp.int32, (blocks, bk_ref.shape[2]), 0)
    tenant = jnp.zeros_like(which)
    for b in range(blocks):
        tenant = jnp.where(which == b, tenants[0, b], tenant)
    hot = lax.broadcasted_iota(jnp.int32, tenant.shape, 1) == tenant
    hot = jnp.where(hot, 1.0, 0.0).astype(BF16)
    for ref, at in ((bk_ref, 32), (bv_ref, 96)):
        flat = ref[...].reshape(rank * cols, ref.shape[2])
        got = lax.dot_general(hot, flat, (((1,), (1,)), ((), ())), preferred_element_type=F32)
        for r in range(rank):
            up[:, r, at : at + cols] = got[:, cols * r : cols * (r + 1)]
    for c in copies:
        c.wait()
    for b in range(blocks):
        at = slice(LANE * b, LANE * (b + 1))
        for i, ref in enumerate((ak, av)):
            low[rank * i : rank * (i + 1), at] = ref[b][:, :LANE]
            low[rank * (2 + i) : rank * (3 + i), LANE * b : LANE * b + feat - LANE] = ref[b][:, LANE:]
    stores[3].start()
    for b in range(blocks):
        a0 = ak[b]
        a1 = av[b]
        main = jnp.concatenate([a0[:, :LANE], a1[:, :LANE]], axis=0)
        near = up[b].astype(BF16)
        tail = jnp.concatenate(
            [a0[:, LANE:], near[:, 32:64], a1[:, LANE:], near[:, 96:128]], axis=1
        )
        for q in range(quad):
            send_ref[quad * b + q, 0:64, :] = main
            send_ref[quad * b + q, 64:96, :] = tail
    for c in stores:
        c.wait()


def lane_mask(rows, slot):
    lane = lax.broadcasted_iota(jnp.int32, (rows, LANE), 1)
    return (lane >= 32 * slot) & (lane < 32 * slot + 32)


def vector_kernel(send_ref, recv_ref, out_ref):
    n_mp = send_ref.shape[0]
    masks = [lane_mask(32, s) for s in (0, 2, 1, 3)]
    total = jnp.zeros((32, LANE), F32)
    zero = jnp.zeros((64, LANE), BF16)
    for m in range(n_mp):
        lhs = jnp.concatenate([send_ref[m, 96:128, :], send_ref[m, 128:160, :]], axis=1)
        main = jnp.concatenate([recv_ref[m, 0:64, :], zero], axis=0)
        tail = recv_ref[m, 64:96, :]
        tails = jnp.concatenate([jnp.where(k, tail, jnp.zeros_like(tail)) for k in masks], axis=0)
        rhs = jnp.concatenate([main, tails], axis=1)
        total += lax.dot_general(lhs, rhs, (((1,), (1,)), ((), ())), preferred_element_type=F32)
    for m in range(n_mp):
        out_ref[m] = total


def split(x):
    hi = x.astype(BF16)
    return hi, (x - hi.astype(F32)).astype(BF16)


def first_blocks(tenants, blocks):
    first = []
    for b in range(blocks):
        f = jnp.int32(b)
        for c in range(b - 1, -1, -1):
            f = jnp.where(tenants[0, c] == tenants[0, b], c, f)
        first.append(f)
    return first


PIECES = (64, 32)
PART = sum(PIECES)


def parts_kernel(where, tenants, vec_ref, recv_ref, top_ref, bottom_ref, low_ref):
    blocks = vec_ref.shape[0] // 4
    m0, m1, m2, m3 = [lane_mask(32, s) for s in range(4)]
    first = first_blocks(tenants, blocks)
    top_ref[...] = jnp.zeros_like(top_ref)
    bottom_ref[...] = jnp.zeros_like(bottom_ref)
    for b in range(blocks):
        vec = vec_ref[4 * b : 4 * b + 4].reshape(BLOCK, LANE) * SCALE
        lhs = jnp.concatenate(split(vec), axis=0)
        near = recv_ref[4 * b : 4 * b + 4, 96:128, :].reshape(BLOCK, LANE)
        far = recv_ref[4 * b : 4 * b + 4, 128:160, :].reshape(BLOCK, LANE)
        rhs = jnp.concatenate([near, far], axis=1)
        rhs = jnp.concatenate([rhs, rhs], axis=0)
        p = lax.dot_general(lhs, rhs, (((0,), (0,)), ((), ())), preferred_element_type=F32)
        q = p[:, LANE:]
        tail = jnp.where(m0, q[64:96], jnp.where(m1, q[0:32], jnp.where(m2, q[96:128], q[32:64])))
        top_ref[pl.ds(pl.multiple_of(first[b] * 64, 8), 64), :] += p[64:128, :LANE]
        bottom_ref[pl.ds(pl.multiple_of(first[b] * 32, 8), 32), :] += tail
    row = lax.broadcasted_iota(jnp.int32, (blocks, LANE), 0)
    ids = jnp.full((blocks, LANE), -1, jnp.int32)
    for b in range(blocks):
        ids = jnp.where((row == b) & (first[b] == b), tenants[0, b], ids)
    top_ref[blocks * 64 :, :] = ids.astype(F32)
    bottom_ref[blocks * 32 :, :] = ids.astype(F32)
    core = where[0] % 2
    for i in range(low_ref.shape[0]):
        back = vec_ref[2 * i + core][:, 64:] * SCALE
        low_ref[i] = jnp.concatenate(split(back), axis=1)


def kept(tenant, parity):
    return (tenant >= 0) & ((tenant // 4) % 2 == parity), (tenant // 8) * 4 + tenant % 4


def piece_of(out_hbm, mine, place, h):
    return out_hbm.at[jnp.where(mine, place, 0), pl.ds(sum(PIECES[:h]), PIECES[h])]


def own_kernel(plane, tenants, top_ref, bottom_ref, out_hbm, zeros, fill_sems, sems):
    blocks = sems.shape[1]
    zeros[...] = jnp.zeros_like(zeros)
    chunk = zeros.shape[0]
    fills = [
        pltpu.make_async_copy(zeros, out_hbm.at[pl.ds(i * chunk, chunk)], fill_sems.at[i])
        for i in range(out_hbm.shape[0] // chunk)
    ]
    for c in fills:
        c.start()
    first = first_blocks(tenants, blocks)
    for c in fills:
        c.wait()
    todo = []
    for b in range(blocks):
        mine, place = kept(tenants[0, b], plane[0] % 2)
        mine = mine & (first[b] == b)
        for h, ref in enumerate((top_ref, bottom_ref)):
            src = ref.at[pl.ds(b * PIECES[h], PIECES[h])]
            dst = piece_of(out_hbm, mine, place, h)
            todo.append((mine, pltpu.make_async_copy(src, dst, sems.at[h, b])))
    for mine, copy in todo:
        pl.when(mine)(copy.start)
    for mine, copy in todo:
        pl.when(mine)(copy.wait)


def merge_kernel(
    plane, tenants, top_ref, bottom_ref, got_top, got_bottom, own_hbm, out_hbm,
    top_buf, bottom_buf, sems,
):
    blocks = sems.shape[1]
    gots = got_top, got_bottom
    todo = []
    for h, (ref, got, buf) in enumerate(zip((top_ref, bottom_ref), gots, (top_buf, bottom_buf))):
        size = PIECES[h]
        for b in range(blocks):
            tenant = got[blocks * size + b, 0].astype(jnp.int32)
            mine, place = kept(tenant, plane[0] % 2)
            same = jnp.int32(-1)
            for c in range(blocks - 1, -1, -1):
                same = jnp.where(tenants[0, c] == tenant, c, same)
            at = pl.multiple_of(jnp.maximum(same, 0) * size, 8)
            here = jnp.where(same >= 0, 1.0, 0.0)
            buf[b] = got[b * size : (b + 1) * size, :] + ref[pl.ds(at, size), :] * here
            copy = pltpu.make_async_copy(buf.at[b], piece_of(out_hbm, mine, place, h), sems.at[h, b])
            pl.when(mine)(copy.start)
            todo.append((mine, copy))
    for mine, copy in todo:
        pl.when(mine)(copy.wait)


def weights_kernel(where, near_hbm, far_hbm, w_ref, a_ref, near_ref, far_ref, sems):
    loads = [
        pltpu.make_async_copy(near_hbm, near_ref, sems.at[0]),
        pltpu.make_async_copy(far_hbm, far_ref, sems.at[1]),
    ]
    for c in loads:
        c.start()
    for c in loads:
        c.wait()
    width = near_ref.shape[1]
    blocks = a_ref.shape[0]
    feat = w_ref.shape[0] // 2
    rank = a_ref.shape[1] // 4
    core = where[0] % 2
    for c, ref in enumerate((near_ref, far_ref)):
        at = pl.multiple_of(jnp.where(core == 0, c, 1 - c) * feat, 16)
        w_ref[pl.ds(at, feat), :width] = ref[0:feat, :]
        w_ref[pl.ds(at, feat), width:] = ref[feat : 2 * feat, :]
    first = 2 * feat
    for b in range(blocks):
        pair = []
        for ref in (near_ref, far_ref):
            main = ref[first : first + 2 * rank, LANE * b : LANE * (b + 1)]
            rest = ref[first + 2 * rank :, LANE * b : LANE * b + feat - LANE]
            pair.append(jnp.concatenate([main, rest], axis=1).astype(F32))
        same, other = jnp.concatenate(pair, axis=1), jnp.concatenate(pair[::-1], axis=1)
        a = jnp.where(core == 0, same, other).astype(BF16)
        a_ref[b, : 2 * rank, :] = a
        a_ref[b, 2 * rank :, :] = a


def base_kernel(kv_ref, w_ref, a_ref, low_ref, out_ref):
    blocks = a_ref.shape[0]
    per = kv_ref.shape[0] // blocks
    step = 4
    for s in range(0, blocks, step):
        rows = [kv_ref[i % 4 * (kv_ref.shape[0] // 4) + i // 4] for i in range(per * s, per * (s + step))]
        rows = jnp.concatenate(rows, axis=0)
        res = lax.dot_general(rows, w_ref[...], (((1,), (1,)), ((), ())), preferred_element_type=F32)
        size = res.shape[0] // step
        for i in range(step):
            b = s + i
            low = low_ref[per * b : per * (b + 1)].reshape(-1, LANE)
            total = res[size * i : size * (i + 1)] + jnp.dot(low, a_ref[b], preferred_element_type=F32)
            out_ref[per * b : per * (b + 1)] = total.astype(BF16).reshape(per, -1, w_ref.shape[0])


def finish_kernel(sum_hbm, ak_ref, av_ref, bk_ref, bv_ref, sum_ref, sem):
    load = pltpu.make_async_copy(sum_hbm, sum_ref, sem)
    load.start()
    load.wait()
    for t in range(sum_ref.shape[0]):
        tail = sum_ref[t, 64:96, :]
        ak_ref[t, :, :LANE] = sum_ref[t, 0:32, :]
        ak_ref[t, :, LANE:] = tail[:, 0:32]
        av_ref[t, :, :LANE] = sum_ref[t, 32:64, :]
        av_ref[t, :, LANE:] = tail[:, 64:96]
        bk_ref[t] = tail[:, 32:64]
        bv_ref[t] = tail[:, 96:128]


def shards(x, kg, vg, wk, wv, ak, av, bk, bv, tenant_of_block, live_token_count):
    mp = ("y", "x", "core")
    n_mp = lax.axis_size(mp)
    tok, width = x.shape
    blocks = tenant_of_block.shape[1]
    feat = wk.shape[0]
    kv_width = kg.shape[1]
    tenants, rank = ak.shape[:2]
    me = lax.axis_index(mp).astype(jnp.int32).reshape(1)
    cols = bk.shape[2]
    hbm = lambda a: pltpu.with_memory_space_constraint(a, pltpu.HBM)
    bundle_rows = 2 * feat + 4 * rank
    send, masked, bundle = pl.pallas_call(
        pack_kernel,
        out_shape=(
            jax.ShapeDtypeStruct((n_mp, 160, LANE), BF16),
            jax.ShapeDtypeStruct((tok, 2 * kv_width), BF16),
            jax.ShapeDtypeStruct((bundle_rows, kv_width), BF16),
        ),
        in_specs=[SMEM] + [HBM] * 11,
        out_specs=(VMEM, HBM, HBM),
        scratch_shapes=[
            pltpu.SMEM((1, blocks), jnp.int32),
            pltpu.SMEM((1, blocks), jnp.int32),
            pltpu.VMEM((tok, width), BF16),
            pltpu.VMEM((tok, kv_width), BF16),
            pltpu.VMEM((tok, kv_width), BF16),
            pltpu.VMEM((rank, cols, tenants), BF16),
            pltpu.VMEM((rank, cols, tenants), BF16),
            pltpu.VMEM((blocks, rank, feat), BF16),
            pltpu.VMEM((blocks, rank, feat), BF16),
            pltpu.VMEM((blocks, rank, LANE), F32),
            pltpu.VMEM((tok, 2 * kv_width), BF16),
            pltpu.VMEM((4 * rank, kv_width), BF16),
            pltpu.SemaphoreType.DMA((7,)),
            pltpu.SemaphoreType.DMA((2, blocks)),
            pltpu.SemaphoreType.DMA((4,)),
        ],
        compiler_params=PARAMS,
        name="pack",
    )(
        me, hbm(tenant_of_block), hbm(live_token_count), hbm(x), hbm(kg), hbm(vg),
        hbm(bk.transpose(1, 2, 0)), hbm(bv.transpose(1, 2, 0)), hbm(ak), hbm(av), hbm(wk), hbm(wv),
    )
    recv = lax.all_to_all(send, mp, split_axis=0, concat_axis=0, tiled=True)
    vec_send = pl.pallas_call(
        vector_kernel,
        out_shape=jax.ShapeDtypeStruct((n_mp, tok, LANE), F32),
        in_specs=[VMEM, VMEM],
        out_specs=VMEM,
        compiler_params=PARAMS,
        name="vectors",
    )(send, recv)
    vec = lax.all_to_all(vec_send, mp, split_axis=0, concat_axis=0, tiled=True)
    groups = [jax.ShapeDtypeStruct((blocks * n + blocks, LANE), F32) for n in PIECES]
    top, bottom, low = pl.pallas_call(
        parts_kernel,
        out_shape=(*groups, jax.ShapeDtypeStruct((n_mp // 2, tok, LANE), BF16)),
        in_specs=[SMEM, SMEM, VMEM, VMEM],
        out_specs=(VMEM, VMEM, VMEM),
        compiler_params=PARAMS,
        name="parts",
    )(me, tenant_of_block, vec, recv)

    dp = ("zh", "zl")
    n_dp = lax.axis_size(dp)
    pairs = [(z, z ^ 1) for z in range(n_dp)]
    others = [(z, (z + (1 if z % 2 else -1)) % n_dp) for z in range(n_dp)]
    got_top = lax.ppermute(top, dp, pairs)
    got_bottom = lax.ppermute(bottom, dp, others)
    plane = lax.axis_index("zl").astype(jnp.int32).reshape(1)
    half = jax.ShapeDtypeStruct((tenants // 2, PART, LANE), F32)
    own = pl.pallas_call(
        own_kernel,
        out_shape=half,
        in_specs=[SMEM, SMEM, VMEM, VMEM],
        out_specs=HBM,
        scratch_shapes=[
            pltpu.VMEM((tenants // 16, PART, LANE), F32),
            pltpu.SemaphoreType.DMA((8,)),
            pltpu.SemaphoreType.DMA((2, blocks)),
        ],
        compiler_params=PARAMS,
        name="own",
    )(plane, tenant_of_block, top, bottom)
    got_top, bundle = lax.optimization_barrier((got_top, bundle))
    far = lax.ppermute(bundle, "core", [(0, 1), (1, 0)])
    sums = pl.pallas_call(
        merge_kernel,
        out_shape=half,
        in_specs=[SMEM, SMEM, VMEM, VMEM, VMEM, VMEM, HBM],
        out_specs=HBM,
        scratch_shapes=[
            *[pltpu.VMEM((blocks, n, LANE), F32) for n in PIECES],
            pltpu.SemaphoreType.DMA((2, blocks)),
        ],
        input_output_aliases={6: 0},
        compiler_params=PARAMS,
        name="merge",
    )(plane, tenant_of_block, top, bottom, got_top, got_bottom, own)

    sums, masked = lax.optimization_barrier((sums, masked))
    sums = lax.psum_scatter(sums, "zh", scatter_dimension=0, tiled=True)

    def swap(a, axes):
        return lax.all_to_all(a, axes, split_axis=0, concat_axis=0, tiled=True)

    kv = swap(jnp.broadcast_to(masked[None], (n_mp // 2, *masked.shape)), ("x", "y"))
    w, a = pl.pallas_call(
        weights_kernel,
        out_shape=(
            pltpu.VMEM((2 * feat, 2 * kv_width), BF16),
            pltpu.VMEM((blocks, 4 * rank, 2 * feat), BF16),
        ),
        in_specs=[SMEM, HBM, HBM],
        out_specs=(VMEM, VMEM),
        scratch_shapes=[
            pltpu.VMEM(bundle.shape, BF16),
            pltpu.VMEM(bundle.shape, BF16),
            pltpu.SemaphoreType.DMA((2,)),
        ],
        compiler_params=PARAMS,
        name="weights",
    )(me, hbm(bundle), hbm(far))
    grad = pl.pallas_call(
        base_kernel,
        out_shape=jax.ShapeDtypeStruct((n_mp // 2, tok, 2 * feat), BF16),
        in_specs=[VMEM] * 4,
        out_specs=VMEM,
        compiler_params=PARAMS,
        name="base",
    )(kv, w, a, low)
    grad = swap(grad, ("y", "x"))
    grad_in = grad.transpose(1, 0, 2).reshape(tok, width)
    sums, grad_in = lax.optimization_barrier((sums, grad_in))

    owned = tenants // lax.axis_size(("zh", "zl"))
    grads = pl.pallas_call(
        finish_kernel,
        out_shape=(
            jax.ShapeDtypeStruct((owned, rank, feat), F32),
            jax.ShapeDtypeStruct((owned, rank, feat), F32),
            jax.ShapeDtypeStruct((owned, rank, bk.shape[2]), F32),
            jax.ShapeDtypeStruct((owned, rank, bk.shape[2]), F32),
        ),
        in_specs=[HBM],
        out_specs=(VMEM, VMEM, VMEM, VMEM),
        scratch_shapes=[pltpu.VMEM((owned, PART, LANE), F32), pltpu.SemaphoreType.DMA],
        compiler_params=PARAMS,
        name="finish",
    )(hbm(sums))
    return (grad_in, *grads)


def solution(mesh):
    n_dp, n_mp = mesh.devices.shape
    fine = Mesh(
        mesh.devices.reshape(n_dp // 2, 2, 4, n_mp // 8, 2), ("zh", "zl", "y", "x", "core")
    )
    dp, mp = ("zh", "zl"), ("y", "x", "core")
    rows = P((*dp, *mp), None)
    in_specs = (
        rows, rows, rows,
        P(mp, None), P(mp, None),
        P(None, None, mp), P(None, None, mp), P(None, None, mp), P(None, None, mp),
        P(dp, None), P(dp, None),
    )
    grads = P(dp, None, mp)
    return jax.shard_map(
        shards, mesh=fine, in_specs=in_specs, out_specs=(rows, grads, grads, grads, grads),
        check_vma=False,
    )
```

```python
import functools

import jax
import jax.numpy as jnp
from jax import lax
from jax.experimental import pallas as pl
from jax.experimental.pallas import tpu as pltpu
from jax.sharding import Mesh, PartitionSpec as P

BLOCK = 128
SCALE = 0.5
F32 = jnp.float32
BF16 = jnp.bfloat16
VMEM = pl.BlockSpec(memory_space=pltpu.VMEM)
SMEM = pl.BlockSpec(memory_space=pltpu.SMEM)
HBM = pl.BlockSpec(memory_space=pltpu.HBM)
PARAMS = pltpu.CompilerParams(vmem_limit_bytes=24 * 1024 * 1024)
LANE = 128

PACKED = 224


def slot(chip):
    return chip % 4 * 4 + chip // 4


def tokens_of(ref, chip, core):
    at = pl.multiple_of(96 + 64 * core, 32)
    return ref[slot(chip), pl.ds(at, 32), :], ref[slot(chip), pl.ds(at + 32, 32), :]


def pack_kernel(
    where, tenants_hbm, counts_hbm, x_hbm, k_hbm, v_hbm, bk_hbm, bv_hbm, ak_hbm, av_hbm, wk_hbm, wv_hbm,
    send_ref, masked_hbm, bundle_hbm,
    tenants, counts, x_ref, k_ref, v_ref, bk_ref, bv_ref, ak, av, up, masked, low, sems, a_sems, out_sems,
):
    n_mp = 2 * send_ref.shape[0]
    blocks, rank, feat = ak.shape
    tok, kv_width = k_ref.shape
    cols = kv_width // n_mp
    quad = n_mp // blocks
    pairs = (
        (tenants_hbm, tenants), (counts_hbm, counts), (x_hbm, x_ref), (k_hbm, k_ref),
        (v_hbm, v_ref), (bk_hbm, bk_ref), (bv_hbm, bv_ref),
    )
    loads = [pltpu.make_async_copy(src, dst, sems.at[i]) for i, (src, dst) in enumerate(pairs)]
    for c in loads:
        c.start()
    feat_rows = pl.ds(0, feat), pl.ds(feat, feat)
    stores = [
        pltpu.make_async_copy(wk_hbm, bundle_hbm.at[feat_rows[0]], out_sems.at[0]),
        pltpu.make_async_copy(wv_hbm, bundle_hbm.at[feat_rows[1]], out_sems.at[1]),
        pltpu.make_async_copy(masked, masked_hbm, out_sems.at[2]),
        pltpu.make_async_copy(low, bundle_hbm.at[pl.ds(2 * feat, low.shape[0])], out_sems.at[3]),
    ]
    stores[0].start()
    stores[1].start()
    loads[0].wait()
    copies = []
    for b in range(blocks):
        t = tenants[0, b]
        copies.append(pltpu.make_async_copy(ak_hbm.at[t], ak.at[b], a_sems.at[0, b]))
        copies.append(pltpu.make_async_copy(av_hbm.at[t], av.at[b], a_sems.at[1, b]))
    for c in copies:
        c.start()
    for c in loads[1:]:
        c.wait()
    me = where[0]
    count = counts[0, me // quad]
    row = lax.broadcasted_iota(jnp.int32, (tok, 1), 0) + (me % quad) * tok
    live = row < count
    mk = jnp.where(live, k_ref[...].astype(F32), 0.0).astype(BF16)
    mv = jnp.where(live, v_ref[...].astype(F32), 0.0).astype(BF16)
    masked[:, :kv_width] = mk
    masked[:, kv_width:] = mv
    stores[2].start()
    x = x_ref[...]
    for j in range(n_mp):
        at = 96 + 64 * (j % 2)
        send_ref[slot(j // 2), at : at + 32, :] = x[:, feat * j : feat * j + LANE]
        last = x[:, feat * j + LANE : feat * (j + 1)]
        send_ref[slot(j // 2), at + 32 : at + 64, :] = jnp.concatenate(
            [last, mk[:, cols * j : cols * (j + 1)], last, mv[:, cols * j : cols * (j + 1)]], axis=1
        )
    which = lax.broadcasted_iota(jnp.int32, (blocks, bk_ref.shape[2]), 0)
    tenant = jnp.zeros_like(which)
    for b in range(blocks):
        tenant = jnp.where(which == b, tenants[0, b], tenant)
    hot = lax.broadcasted_iota(jnp.int32, tenant.shape, 1) == tenant
    hot = jnp.where(hot, 1.0, 0.0).astype(BF16)
    for ref, at in ((bk_ref, 32), (bv_ref, 96)):
        flat = ref[...].reshape(rank * cols, ref.shape[2])
        got = lax.dot_general(hot, flat, (((1,), (1,)), ((), ())), preferred_element_type=F32)
        for r in range(rank):
            up[:, r, at : at + cols] = got[:, cols * r : cols * (r + 1)]
    for c in copies:
        c.wait()
    for b in range(blocks):
        at = slice(LANE * b, LANE * (b + 1))
        for i, ref in enumerate((ak, av)):
            low[rank * i : rank * (i + 1), at] = ref[b][:, :LANE]
            low[rank * (2 + i) : rank * (3 + i), LANE * b : LANE * b + feat - LANE] = ref[b][:, LANE:]
    stores[3].start()
    for b in range(blocks):
        a0 = ak[b]
        a1 = av[b]
        main = jnp.concatenate([a0[:, :LANE], a1[:, :LANE]], axis=0)
        near = up[b].astype(BF16)
        tail = jnp.concatenate(
            [a0[:, LANE:], near[:, 32:64], a1[:, LANE:], near[:, 96:128]], axis=1
        )
        for q in range(quad // 2):
            send_ref[slot(quad // 2 * b + q), 0:64, :] = main
            send_ref[slot(quad // 2 * b + q), 64:96, :] = tail
    for c in stores:
        c.wait()


def lane_mask(rows, slot):
    lane = lax.broadcasted_iota(jnp.int32, (rows, LANE), 1)
    return (lane >= 32 * slot) & (lane < 32 * slot + 32)


def vector_kernel(where, send_ref, recv_ref, other_ref, out_ref):
    core = where[0] % 2
    masks = [lane_mask(32, s) for s in (0, 2, 1, 3)]
    total = jnp.zeros((32, LANE), F32)
    zero = jnp.zeros((64, LANE), BF16)
    for chip in range(send_ref.shape[0]):
        for ref, c in ((recv_ref, core), (other_ref, 1 - core)):
            lhs = jnp.concatenate(tokens_of(send_ref, chip, c), axis=1)
            main = jnp.concatenate([ref[slot(chip), 0:64, :], zero], axis=0)
            tail = ref[slot(chip), 64:96, :]
            tails = jnp.concatenate([jnp.where(k, tail, jnp.zeros_like(tail)) for k in masks], axis=0)
            rhs = jnp.concatenate([main, tails], axis=1)
            total += lax.dot_general(lhs, rhs, (((1,), (1,)), ((), ())), preferred_element_type=F32)
    for m in range(out_ref.shape[0]):
        out_ref[m] = total


def split(x):
    hi = x.astype(BF16)
    return hi, (x - hi.astype(F32)).astype(BF16)


def first_blocks(tenants, blocks):
    first = []
    for b in range(blocks):
        f = jnp.int32(b)
        for c in range(b - 1, -1, -1):
            f = jnp.where(tenants[0, c] == tenants[0, b], c, f)
        first.append(f)
    return first


PIECES = (64, 32)
PART = sum(PIECES)


def parts_kernel(where, tenants, vec_ref, recv_ref, other_ref, top_ref, bottom_ref, low_ref):
    core = where[0] % 2
    blocks = vec_ref.shape[0] // 4
    m0, m1, m2, m3 = [lane_mask(32, s) for s in range(4)]
    first = first_blocks(tenants, blocks)
    top_ref[...] = jnp.zeros_like(top_ref)
    bottom_ref[...] = jnp.zeros_like(bottom_ref)
    for b in range(blocks):
        vec, near, far = [], [], []
        for chip in (2 * b, 2 * b + 1):
            for ref, c in ((recv_ref, core), (other_ref, 1 - core)):
                vec.append(vec_ref[2 * chip + c] * SCALE)
                first_part, last_part = tokens_of(ref, chip, core)
                near.append(first_part)
                far.append(last_part)
        lhs = jnp.concatenate(split(jnp.concatenate(vec, axis=0)), axis=0)
        near = jnp.concatenate(near, axis=0)
        far = jnp.concatenate(far, axis=0)
        rhs = jnp.concatenate([near, far], axis=1)
        rhs = jnp.concatenate([rhs, rhs], axis=0)
        p = lax.dot_general(lhs, rhs, (((0,), (0,)), ((), ())), preferred_element_type=F32)
        q = p[:, LANE:]
        tail = jnp.where(m0, q[64:96], jnp.where(m1, q[0:32], jnp.where(m2, q[96:128], q[32:64])))
        top_ref[pl.ds(pl.multiple_of(first[b] * 64, 8), 64), :] += p[64:128, :LANE]
        bottom_ref[pl.ds(pl.multiple_of(first[b] * 32, 8), 32), :] += tail
    row = lax.broadcasted_iota(jnp.int32, (blocks, LANE), 0)
    ids = jnp.full((blocks, LANE), -1, jnp.int32)
    for b in range(blocks):
        ids = jnp.where((row == b) & (first[b] == b), tenants[0, b], ids)
    top_ref[blocks * 64 :, :] = ids.astype(F32)
    bottom_ref[blocks * 32 :, :] = ids.astype(F32)
    for i in range(low_ref.shape[0]):
        back = vec_ref[2 * i + core][:, 64:] * SCALE
        low_ref[i] = jnp.concatenate(split(back), axis=1)


def kept(tenant, parity):
    return (tenant >= 0) & ((tenant // 4) % 2 == parity), (tenant // 8) * 4 + tenant % 4


def piece_of(out_hbm, mine, place, h):
    return out_hbm.at[jnp.where(mine, place, 0), pl.ds(sum(PIECES[:h]), PIECES[h])]


def own_kernel(plane, tenants, top_ref, bottom_ref, out_hbm, zeros, fill_sems, sems):
    blocks = sems.shape[1]
    zeros[...] = jnp.zeros_like(zeros)
    chunk = zeros.shape[0]
    fills = [
        pltpu.make_async_copy(zeros, out_hbm.at[pl.ds(i * chunk, chunk)], fill_sems.at[i])
        for i in range(out_hbm.shape[0] // chunk)
    ]
    for c in fills:
        c.start()
    first = first_blocks(tenants, blocks)
    for c in fills:
        c.wait()
    todo = []
    for b in range(blocks):
        mine, place = kept(tenants[0, b], plane[0] % 2)
        mine = mine & (first[b] == b)
        for h, ref in enumerate((top_ref, bottom_ref)):
            src = ref.at[pl.ds(b * PIECES[h], PIECES[h])]
            dst = piece_of(out_hbm, mine, place, h)
            todo.append((mine, pltpu.make_async_copy(src, dst, sems.at[h, b])))
    for mine, copy in todo:
        pl.when(mine)(copy.start)
    for mine, copy in todo:
        pl.when(mine)(copy.wait)


def merge_kernel(
    plane, tenants, top_ref, bottom_ref, got_top, got_bottom, own_hbm, out_hbm,
    top_buf, bottom_buf, sems,
):
    blocks = sems.shape[1]
    gots = got_top, got_bottom
    todo = []
    for h, (ref, got, buf) in enumerate(zip((top_ref, bottom_ref), gots, (top_buf, bottom_buf))):
        size = PIECES[h]
        for b in range(blocks):
            tenant = got[blocks * size + b, 0].astype(jnp.int32)
            mine, place = kept(tenant, plane[0] % 2)
            same = jnp.int32(-1)
            for c in range(blocks - 1, -1, -1):
                same = jnp.where(tenants[0, c] == tenant, c, same)
            at = pl.multiple_of(jnp.maximum(same, 0) * size, 8)
            here = jnp.where(same >= 0, 1.0, 0.0)
            buf[b] = got[b * size : (b + 1) * size, :] + ref[pl.ds(at, size), :] * here
            copy = pltpu.make_async_copy(buf.at[b], piece_of(out_hbm, mine, place, h), sems.at[h, b])
            pl.when(mine)(copy.start)
            todo.append((mine, copy))
    for mine, copy in todo:
        pl.when(mine)(copy.wait)


def weights_kernel(where, near_ref, far_ref, w_ref, a_ref):
    width = near_ref.shape[1]
    blocks = a_ref.shape[0]
    feat = w_ref.shape[0] // 2
    rank = a_ref.shape[1] // 4
    core = where[0] % 2
    for c, ref in enumerate((near_ref, far_ref)):
        at = pl.multiple_of(jnp.where(core == 0, c, 1 - c) * feat, 16)
        w_ref[pl.ds(at, feat), :width] = ref[0:feat, :]
        w_ref[pl.ds(at, feat), width:] = ref[feat : 2 * feat, :]
    first = 2 * feat
    for b in range(blocks):
        pair = []
        for ref in (near_ref, far_ref):
            main = ref[first : first + 2 * rank, LANE * b : LANE * (b + 1)]
            rest = ref[first + 2 * rank :, LANE * b : LANE * b + feat - LANE]
            pair.append(jnp.concatenate([main, rest], axis=1).astype(F32))
        same, other = jnp.concatenate(pair, axis=1), jnp.concatenate(pair[::-1], axis=1)
        a = jnp.where(core == 0, same, other).astype(BF16)
        a_ref[b, : 2 * rank, :] = a
        a_ref[b, 2 * rank :, :] = a


def base_kernel(kv_ref, w_ref, a_hbm, low_ref, out_ref, a_ref, sem):
    load = pltpu.make_async_copy(a_hbm, a_ref, sem)
    load.start()
    blocks = a_ref.shape[0]
    per = kv_ref.shape[0] // blocks
    step = 4
    for s in range(0, blocks, step):
        rows = [kv_ref[i % 4 * (kv_ref.shape[0] // 4) + i // 4] for i in range(per * s, per * (s + step))]
        rows = jnp.concatenate(rows, axis=0)
        res = lax.dot_general(rows, w_ref[...], (((1,), (1,)), ((), ())), preferred_element_type=F32)
        size = res.shape[0] // step
        if s == 0:
            load.wait()
        for i in range(step):
            b = s + i
            low = low_ref[per * b : per * (b + 1)].reshape(-1, LANE)
            total = res[size * i : size * (i + 1)] + jnp.dot(low, a_ref[b], preferred_element_type=F32)
            out_ref[per * b : per * (b + 1)] = total.astype(BF16).reshape(per, -1, w_ref.shape[0])


def finish_kernel(sum_hbm, ak_ref, av_ref, bk_ref, bv_ref, sum_ref, sem):
    load = pltpu.make_async_copy(sum_hbm, sum_ref, sem)
    load.start()
    load.wait()
    for t in range(sum_ref.shape[0]):
        tail = sum_ref[t, 64:96, :]
        ak_ref[t, :, :LANE] = sum_ref[t, 0:32, :]
        ak_ref[t, :, LANE:] = tail[:, 0:32]
        av_ref[t, :, :LANE] = sum_ref[t, 32:64, :]
        av_ref[t, :, LANE:] = tail[:, 64:96]
        bk_ref[t] = tail[:, 32:64]
        bv_ref[t] = tail[:, 96:128]


def shards(x, kg, vg, wk, wv, ak, av, bk, bv, tenant_of_block, live_token_count):
    mp = ("y", "x", "core")
    n_mp = lax.axis_size(mp)
    tok, width = x.shape
    blocks = tenant_of_block.shape[1]
    feat = wk.shape[0]
    kv_width = kg.shape[1]
    tenants, rank = ak.shape[:2]
    me = lax.axis_index(mp).astype(jnp.int32).reshape(1)
    cols = bk.shape[2]
    hbm = lambda a: pltpu.with_memory_space_constraint(a, pltpu.HBM)
    bundle_rows = 2 * feat + 4 * rank
    send, masked, bundle = pl.pallas_call(
        pack_kernel,
        out_shape=(
            jax.ShapeDtypeStruct((n_mp // 2, PACKED, LANE), BF16),
            jax.ShapeDtypeStruct((tok, 2 * kv_width), BF16),
            jax.ShapeDtypeStruct((bundle_rows, kv_width), BF16),
        ),
        in_specs=[SMEM] + [HBM] * 11,
        out_specs=(VMEM, HBM, HBM),
        scratch_shapes=[
            pltpu.SMEM((1, blocks), jnp.int32),
            pltpu.SMEM((1, blocks), jnp.int32),
            pltpu.VMEM((tok, width), BF16),
            pltpu.VMEM((tok, kv_width), BF16),
            pltpu.VMEM((tok, kv_width), BF16),
            pltpu.VMEM((rank, cols, tenants), BF16),
            pltpu.VMEM((rank, cols, tenants), BF16),
            pltpu.VMEM((blocks, rank, feat), BF16),
            pltpu.VMEM((blocks, rank, feat), BF16),
            pltpu.VMEM((blocks, rank, LANE), F32),
            pltpu.VMEM((tok, 2 * kv_width), BF16),
            pltpu.VMEM((4 * rank, kv_width), BF16),
            pltpu.SemaphoreType.DMA((7,)),
            pltpu.SemaphoreType.DMA((2, blocks)),
            pltpu.SemaphoreType.DMA((4,)),
        ],
        compiler_params=PARAMS,
        name="pack",
    )(
        me, hbm(tenant_of_block), hbm(live_token_count), hbm(x), hbm(kg), hbm(vg),
        hbm(bk.transpose(1, 2, 0)), hbm(bv.transpose(1, 2, 0)), hbm(ak), hbm(av), hbm(wk), hbm(wv),
    )
    recv = lax.all_to_all(send, ("x", "y"), split_axis=0, concat_axis=0, tiled=True)
    siblings = [(0, 1), (1, 0)]
    other = lax.ppermute(recv, "core", siblings)
    vec_send = pl.pallas_call(
        vector_kernel,
        out_shape=jax.ShapeDtypeStruct((n_mp, tok, LANE), F32),
        in_specs=[SMEM, VMEM, VMEM, VMEM],
        out_specs=VMEM,
        compiler_params=PARAMS,
        name="vectors",
    )(me, send, recv, other)
    vec = lax.all_to_all(vec_send, mp, split_axis=0, concat_axis=0, tiled=True)
    groups = [jax.ShapeDtypeStruct((blocks * n + blocks, LANE), F32) for n in PIECES]
    top, bottom, low = pl.pallas_call(
        parts_kernel,
        out_shape=(*groups, jax.ShapeDtypeStruct((n_mp // 2, tok, LANE), BF16)),
        in_specs=[SMEM, SMEM, VMEM, VMEM, VMEM],
        out_specs=(VMEM, VMEM, VMEM),
        compiler_params=PARAMS,
        name="parts",
    )(me, tenant_of_block, vec, recv, other)

    dp = ("zh", "zl")
    n_dp = lax.axis_size(dp)
    pairs = [(z, z ^ 1) for z in range(n_dp)]
    others = [(z, (z + (1 if z % 2 else -1)) % n_dp) for z in range(n_dp)]
    got_top = lax.ppermute(top, dp, pairs)
    got_bottom = lax.ppermute(bottom, dp, others)
    plane = lax.axis_index("zl").astype(jnp.int32).reshape(1)
    half = jax.ShapeDtypeStruct((tenants // 2, PART, LANE), F32)
    own = pl.pallas_call(
        own_kernel,
        out_shape=half,
        in_specs=[SMEM, SMEM, VMEM, VMEM],
        out_specs=HBM,
        scratch_shapes=[
            pltpu.VMEM((tenants // 16, PART, LANE), F32),
            pltpu.SemaphoreType.DMA((8,)),
            pltpu.SemaphoreType.DMA((2, blocks)),
        ],
        compiler_params=PARAMS,
        name="own",
    )(plane, tenant_of_block, top, bottom)
    got_top, bundle = lax.optimization_barrier((got_top, bundle))
    far = lax.ppermute(bundle, "core", siblings)
    sums = pl.pallas_call(
        merge_kernel,
        out_shape=half,
        in_specs=[SMEM, SMEM, VMEM, VMEM, VMEM, VMEM, HBM],
        out_specs=HBM,
        scratch_shapes=[
            *[pltpu.VMEM((blocks, n, LANE), F32) for n in PIECES],
            pltpu.SemaphoreType.DMA((2, blocks)),
        ],
        input_output_aliases={6: 0},
        compiler_params=PARAMS,
        name="merge",
    )(plane, tenant_of_block, top, bottom, got_top, got_bottom, own)

    sums, masked = lax.optimization_barrier((sums, masked))
    sums = lax.psum_scatter(sums, "zh", scatter_dimension=0, tiled=True)

    def swap(a, axes):
        return lax.all_to_all(a, axes, split_axis=0, concat_axis=0, tiled=True)

    kv = swap(jnp.broadcast_to(masked[None], (n_mp // 2, *masked.shape)), ("x", "y"))
    w, a = pl.pallas_call(
        weights_kernel,
        out_shape=(
            pltpu.VMEM((2 * feat, 2 * kv_width), BF16),
            jax.ShapeDtypeStruct((blocks, 4 * rank, 2 * feat), BF16),
        ),
        in_specs=[SMEM, VMEM, VMEM],
        out_specs=(VMEM, VMEM),
        compiler_params=PARAMS,
        name="weights",
    )(me, bundle, far)
    grad = pl.pallas_call(
        base_kernel,
        out_shape=jax.ShapeDtypeStruct((n_mp // 2, tok, 2 * feat), BF16),
        in_specs=[VMEM, VMEM, HBM, VMEM],
        out_specs=VMEM,
        scratch_shapes=[pltpu.VMEM(a.shape, BF16), pltpu.SemaphoreType.DMA],
        compiler_params=PARAMS,
        name="base",
    )(kv, w, hbm(a), low)
    grad = swap(grad, ("y", "x"))
    grad_in = grad.transpose(1, 0, 2).reshape(tok, width)
    sums, grad_in = lax.optimization_barrier((sums, grad_in))

    owned = tenants // lax.axis_size(("zh", "zl"))
    grads = pl.pallas_call(
        finish_kernel,
        out_shape=(
            jax.ShapeDtypeStruct((owned, rank, feat), F32),
            jax.ShapeDtypeStruct((owned, rank, feat), F32),
            jax.ShapeDtypeStruct((owned, rank, bk.shape[2]), F32),
            jax.ShapeDtypeStruct((owned, rank, bk.shape[2]), F32),
        ),
        in_specs=[HBM],
        out_specs=(VMEM, VMEM, VMEM, VMEM),
        scratch_shapes=[pltpu.VMEM((owned, PART, LANE), F32), pltpu.SemaphoreType.DMA],
        compiler_params=PARAMS,
        name="finish",
    )(hbm(sums))
    return (grad_in, *grads)


def solution(mesh):
    n_dp, n_mp = mesh.devices.shape
    fine = Mesh(
        mesh.devices.reshape(n_dp // 2, 2, 4, n_mp // 8, 2), ("zh", "zl", "y", "x", "core")
    )
    dp, mp = ("zh", "zl"), ("y", "x", "core")
    rows = P((*dp, *mp), None)
    in_specs = (
        rows, rows, rows,
        P(mp, None), P(mp, None),
        P(None, None, mp), P(None, None, mp), P(None, None, mp), P(None, None, mp),
        P(dp, None), P(dp, None),
    )
    grads = P(dp, None, mp)
    return jax.shard_map(
        shards, mesh=fine, in_specs=in_specs, out_specs=(rows, grads, grads, grads, grads),
        check_vma=False,
    )
```

```python
import functools

import jax
import jax.numpy as jnp
from jax import lax
from jax.experimental import pallas as pl
from jax.experimental.pallas import tpu as pltpu
from jax.sharding import Mesh, PartitionSpec as P

BLOCK = 128
SCALE = 0.5
F32 = jnp.float32
BF16 = jnp.bfloat16
VMEM = pl.BlockSpec(memory_space=pltpu.VMEM)
SMEM = pl.BlockSpec(memory_space=pltpu.SMEM)
HBM = pl.BlockSpec(memory_space=pltpu.HBM)
PARAMS = pltpu.CompilerParams(vmem_limit_bytes=24 * 1024 * 1024)
LANE = 128

PACKED = 224


def slot(chip):
    return chip % 4 * 4 + chip // 4


def tokens_of(ref, chip, core):
    at = pl.multiple_of(96 + 64 * core, 32)
    return ref[slot(chip), pl.ds(at, 32), :], ref[slot(chip), pl.ds(at + 32, 32), :]


def pack_kernel(
    where, tenants_hbm, counts_hbm, x_hbm, k_hbm, v_hbm, bk_hbm, bv_hbm, ak_hbm, av_hbm, wk_hbm, wv_hbm,
    send_ref, masked_hbm, bundle_hbm,
    tenants, counts, x_ref, k_ref, v_ref, bk_ref, bv_ref, ak, av, up, masked, low, sems, a_sems, out_sems,
):
    n_mp = 2 * send_ref.shape[0]
    blocks, rank, feat = ak.shape
    tok, kv_width = k_ref.shape
    cols = kv_width // n_mp
    quad = n_mp // blocks
    pairs = (
        (tenants_hbm, tenants), (counts_hbm, counts), (x_hbm, x_ref), (k_hbm, k_ref),
        (v_hbm, v_ref), (bk_hbm, bk_ref), (bv_hbm, bv_ref),
    )
    loads = [pltpu.make_async_copy(src, dst, sems.at[i]) for i, (src, dst) in enumerate(pairs)]
    for c in loads:
        c.start()
    feat_rows = pl.ds(0, feat), pl.ds(feat, feat)
    stores = [
        pltpu.make_async_copy(wk_hbm, bundle_hbm.at[feat_rows[0]], out_sems.at[0]),
        pltpu.make_async_copy(wv_hbm, bundle_hbm.at[feat_rows[1]], out_sems.at[1]),
        pltpu.make_async_copy(masked, masked_hbm, out_sems.at[2]),
        pltpu.make_async_copy(low, bundle_hbm.at[pl.ds(2 * feat, low.shape[0])], out_sems.at[3]),
    ]
    loads[0].wait()
    copies = []
    for b in range(blocks):
        t = tenants[0, b]
        copies.append(pltpu.make_async_copy(ak_hbm.at[t], ak.at[b], a_sems.at[0, b]))
        copies.append(pltpu.make_async_copy(av_hbm.at[t], av.at[b], a_sems.at[1, b]))
    for c in copies:
        c.start()
    stores[0].start()
    stores[1].start()
    loads[2].wait()
    x = x_ref[...]
    for j in range(n_mp):
        at = 96 + 64 * (j % 2)
        send_ref[slot(j // 2), at : at + 32, :] = x[:, feat * j : feat * j + LANE]
    for i in (1, 3, 4):
        loads[i].wait()
    me = where[0]
    count = counts[0, me // quad]
    row = lax.broadcasted_iota(jnp.int32, (tok, 1), 0) + (me % quad) * tok
    live = row < count
    mk = jnp.where(live, k_ref[...].astype(F32), 0.0).astype(BF16)
    mv = jnp.where(live, v_ref[...].astype(F32), 0.0).astype(BF16)
    masked[:, :kv_width] = mk
    masked[:, kv_width:] = mv
    stores[2].start()
    for j in range(n_mp):
        at = 128 + 64 * (j % 2)
        last = x[:, feat * j + LANE : feat * (j + 1)]
        send_ref[slot(j // 2), at : at + 32, :] = jnp.concatenate(
            [last, mk[:, cols * j : cols * (j + 1)], last, mv[:, cols * j : cols * (j + 1)]], axis=1
        )
    for i in (5, 6):
        loads[i].wait()
    which = lax.broadcasted_iota(jnp.int32, (blocks, bk_ref.shape[2]), 0)
    tenant = jnp.zeros_like(which)
    for b in range(blocks):
        tenant = jnp.where(which == b, tenants[0, b], tenant)
    hot = lax.broadcasted_iota(jnp.int32, tenant.shape, 1) == tenant
    hot = jnp.where(hot, 1.0, 0.0).astype(BF16)
    for ref, at in ((bk_ref, 32), (bv_ref, 96)):
        flat = ref[...].reshape(rank * cols, ref.shape[2])
        got = lax.dot_general(hot, flat, (((1,), (1,)), ((), ())), preferred_element_type=F32)
        for r in range(rank):
            up[:, r, at : at + cols] = got[:, cols * r : cols * (r + 1)]
    for c in copies:
        c.wait()
    for b in range(blocks):
        at = slice(LANE * b, LANE * (b + 1))
        for i, ref in enumerate((ak, av)):
            low[rank * i : rank * (i + 1), at] = ref[b][:, :LANE]
            low[rank * (2 + i) : rank * (3 + i), LANE * b : LANE * b + feat - LANE] = ref[b][:, LANE:]
    stores[3].start()
    for b in range(blocks):
        a0 = ak[b]
        a1 = av[b]
        main = jnp.concatenate([a0[:, :LANE], a1[:, :LANE]], axis=0)
        near = up[b].astype(BF16)
        tail = jnp.concatenate(
            [a0[:, LANE:], near[:, 32:64], a1[:, LANE:], near[:, 96:128]], axis=1
        )
        for q in range(quad // 2):
            send_ref[slot(quad // 2 * b + q), 0:64, :] = main
            send_ref[slot(quad // 2 * b + q), 64:96, :] = tail
    for c in stores:
        c.wait()


def lane_mask(rows, slot):
    lane = lax.broadcasted_iota(jnp.int32, (rows, LANE), 1)
    return (lane >= 32 * slot) & (lane < 32 * slot + 32)


def vectors_of(send_ref, ref, core):
    masks = [lane_mask(32, s) for s in (0, 2, 1, 3)]
    total = jnp.zeros((32, LANE), F32)
    zero = jnp.zeros((64, LANE), BF16)
    for chip in range(send_ref.shape[0]):
        lhs = jnp.concatenate(tokens_of(send_ref, chip, core), axis=1)
        main = jnp.concatenate([ref[slot(chip), 0:64, :], zero], axis=0)
        tail = ref[slot(chip), 64:96, :]
        tails = jnp.concatenate([jnp.where(k, tail, jnp.zeros_like(tail)) for k in masks], axis=0)
        rhs = jnp.concatenate([main, tails], axis=1)
        total += lax.dot_general(lhs, rhs, (((1,), (1,)), ((), ())), preferred_element_type=F32)
    return total


def half_kernel(where, send_ref, recv_ref, out_ref):
    out_ref[...] = vectors_of(send_ref, recv_ref, where[0] % 2)


def vector_kernel(where, send_ref, other_ref, half_ref, out_ref):
    total = half_ref[...] + vectors_of(send_ref, other_ref, 1 - where[0] % 2)
    for m in range(out_ref.shape[0]):
        out_ref[m] = total


def split(x):
    hi = x.astype(BF16)
    return hi, (x - hi.astype(F32)).astype(BF16)


def first_blocks(tenants, blocks):
    first = []
    for b in range(blocks):
        f = jnp.int32(b)
        for c in range(b - 1, -1, -1):
            f = jnp.where(tenants[0, c] == tenants[0, b], c, f)
        first.append(f)
    return first


PIECES = (64, 32)
PART = sum(PIECES)


def parts_kernel(where, tenants, vec_ref, recv_ref, other_ref, top_ref, bottom_ref, low_ref):
    core = where[0] % 2
    blocks = vec_ref.shape[0] // 4
    m0, m1, m2, m3 = [lane_mask(32, s) for s in range(4)]
    first = first_blocks(tenants, blocks)
    top_ref[...] = jnp.zeros_like(top_ref)
    bottom_ref[...] = jnp.zeros_like(bottom_ref)
    for b in range(blocks):
        vec, near, far = [], [], []
        for chip in (2 * b, 2 * b + 1):
            for ref, c in ((recv_ref, core), (other_ref, 1 - core)):
                vec.append(vec_ref[2 * chip + c] * SCALE)
                first_part, last_part = tokens_of(ref, chip, core)
                near.append(first_part)
                far.append(last_part)
        lhs = jnp.concatenate(split(jnp.concatenate(vec, axis=0)), axis=0)
        near = jnp.concatenate(near, axis=0)
        far = jnp.concatenate(far, axis=0)
        rhs = jnp.concatenate([near, far], axis=1)
        rhs = jnp.concatenate([rhs, rhs], axis=0)
        p = lax.dot_general(lhs, rhs, (((0,), (0,)), ((), ())), preferred_element_type=F32)
        q = p[:, LANE:]
        tail = jnp.where(m0, q[64:96], jnp.where(m1, q[0:32], jnp.where(m2, q[96:128], q[32:64])))
        top_ref[pl.ds(pl.multiple_of(first[b] * 64, 8), 64), :] += p[64:128, :LANE]
        bottom_ref[pl.ds(pl.multiple_of(first[b] * 32, 8), 32), :] += tail
    row = lax.broadcasted_iota(jnp.int32, (blocks, LANE), 0)
    ids = jnp.full((blocks, LANE), -1, jnp.int32)
    for b in range(blocks):
        ids = jnp.where((row == b) & (first[b] == b), tenants[0, b], ids)
    top_ref[blocks * 64 :, :] = ids.astype(F32)
    bottom_ref[blocks * 32 :, :] = ids.astype(F32)
    for i in range(low_ref.shape[0]):
        back = vec_ref[2 * i + core][:, 64:] * SCALE
        low_ref[i] = jnp.concatenate(split(back), axis=1)


def kept(tenant, parity):
    return (tenant >= 0) & ((tenant // 4) % 2 == parity), (tenant // 8) * 4 + tenant % 4


def piece_of(out_hbm, mine, place, h):
    return out_hbm.at[jnp.where(mine, place, 0), pl.ds(sum(PIECES[:h]), PIECES[h])]


def own_kernel(plane, tenants, top_ref, bottom_ref, out_hbm, zeros, fill_sems, sems):
    blocks = sems.shape[1]
    zeros[...] = jnp.zeros_like(zeros)
    chunk = zeros.shape[0]
    fills = [
        pltpu.make_async_copy(zeros, out_hbm.at[pl.ds(i * chunk, chunk)], fill_sems.at[i])
        for i in range(out_hbm.shape[0] // chunk)
    ]
    for c in fills:
        c.start()
    first = first_blocks(tenants, blocks)
    for c in fills:
        c.wait()
    todo = []
    for b in range(blocks):
        mine, place = kept(tenants[0, b], plane[0] % 2)
        mine = mine & (first[b] == b)
        for h, ref in enumerate((top_ref, bottom_ref)):
            src = ref.at[pl.ds(b * PIECES[h], PIECES[h])]
            dst = piece_of(out_hbm, mine, place, h)
            todo.append((mine, pltpu.make_async_copy(src, dst, sems.at[h, b])))
    for mine, copy in todo:
        pl.when(mine)(copy.start)
    for mine, copy in todo:
        pl.when(mine)(copy.wait)


def merge_kernel(
    plane, tenants, top_ref, bottom_ref, got_top, got_bottom, own_hbm, out_hbm,
    top_buf, bottom_buf, sems,
):
    blocks = sems.shape[1]
    gots = got_top, got_bottom
    todo = []
    for h, (ref, got, buf) in enumerate(zip((top_ref, bottom_ref), gots, (top_buf, bottom_buf))):
        size = PIECES[h]
        for b in range(blocks):
            tenant = got[blocks * size + b, 0].astype(jnp.int32)
            mine, place = kept(tenant, plane[0] % 2)
            same = jnp.int32(-1)
            for c in range(blocks - 1, -1, -1):
                same = jnp.where(tenants[0, c] == tenant, c, same)
            at = pl.multiple_of(jnp.maximum(same, 0) * size, 8)
            here = jnp.where(same >= 0, 1.0, 0.0)
            buf[b] = got[b * size : (b + 1) * size, :] + ref[pl.ds(at, size), :] * here
            copy = pltpu.make_async_copy(buf.at[b], piece_of(out_hbm, mine, place, h), sems.at[h, b])
            pl.when(mine)(copy.start)
            todo.append((mine, copy))
    for mine, copy in todo:
        pl.when(mine)(copy.wait)


def weights_kernel(where, near_ref, far_ref, w_ref, a_ref):
    width = near_ref.shape[1]
    blocks = a_ref.shape[0]
    feat = w_ref.shape[0] // 2
    rank = a_ref.shape[1] // 4
    core = where[0] % 2
    for c, ref in enumerate((near_ref, far_ref)):
        at = pl.multiple_of(jnp.where(core == 0, c, 1 - c) * feat, 16)
        w_ref[pl.ds(at, feat), :width] = ref[0:feat, :]
        w_ref[pl.ds(at, feat), width:] = ref[feat : 2 * feat, :]
    first = 2 * feat
    for b in range(blocks):
        pair = []
        for ref in (near_ref, far_ref):
            main = ref[first : first + 2 * rank, LANE * b : LANE * (b + 1)]
            rest = ref[first + 2 * rank :, LANE * b : LANE * b + feat - LANE]
            pair.append(jnp.concatenate([main, rest], axis=1).astype(F32))
        same, other = jnp.concatenate(pair, axis=1), jnp.concatenate(pair[::-1], axis=1)
        a = jnp.where(core == 0, same, other).astype(BF16)
        a_ref[b, : 2 * rank, :] = a
        a_ref[b, 2 * rank :, :] = a


def base_kernel(kv_ref, w_ref, a_hbm, low_ref, out_ref, a_ref, sem):
    load = pltpu.make_async_copy(a_hbm, a_ref, sem)
    load.start()
    blocks = a_ref.shape[0]
    per = kv_ref.shape[0] // blocks
    step = 4
    for s in range(0, blocks, step):
        rows = [kv_ref[i % 4 * (kv_ref.shape[0] // 4) + i // 4] for i in range(per * s, per * (s + step))]
        rows = jnp.concatenate(rows, axis=0)
        res = lax.dot_general(rows, w_ref[...], (((1,), (1,)), ((), ())), preferred_element_type=F32)
        size = res.shape[0] // step
        if s == 0:
            load.wait()
        for i in range(step):
            b = s + i
            low = low_ref[per * b : per * (b + 1)].reshape(-1, LANE)
            total = res[size * i : size * (i + 1)] + jnp.dot(low, a_ref[b], preferred_element_type=F32)
            out_ref[per * b : per * (b + 1)] = total.astype(BF16).reshape(per, -1, w_ref.shape[0])


def finish_kernel(sum_hbm, ak_ref, av_ref, bk_ref, bv_ref, sum_ref, sem):
    load = pltpu.make_async_copy(sum_hbm, sum_ref, sem)
    load.start()
    load.wait()
    for t in range(sum_ref.shape[0]):
        tail = sum_ref[t, 64:96, :]
        ak_ref[t, :, :LANE] = sum_ref[t, 0:32, :]
        ak_ref[t, :, LANE:] = tail[:, 0:32]
        av_ref[t, :, :LANE] = sum_ref[t, 32:64, :]
        av_ref[t, :, LANE:] = tail[:, 64:96]
        bk_ref[t] = tail[:, 32:64]
        bv_ref[t] = tail[:, 96:128]


def shards(x, kg, vg, wk, wv, ak, av, bk, bv, tenant_of_block, live_token_count):
    mp = ("y", "x", "core")
    n_mp = lax.axis_size(mp)
    tok, width = x.shape
    blocks = tenant_of_block.shape[1]
    feat = wk.shape[0]
    kv_width = kg.shape[1]
    tenants, rank = ak.shape[:2]
    me = lax.axis_index(mp).astype(jnp.int32).reshape(1)
    cols = bk.shape[2]
    hbm = lambda a: pltpu.with_memory_space_constraint(a, pltpu.HBM)
    bundle_rows = 2 * feat + 4 * rank
    send, masked, bundle = pl.pallas_call(
        pack_kernel,
        out_shape=(
            jax.ShapeDtypeStruct((n_mp // 2, PACKED, LANE), BF16),
            jax.ShapeDtypeStruct((tok, 2 * kv_width), BF16),
            jax.ShapeDtypeStruct((bundle_rows, kv_width), BF16),
        ),
        in_specs=[SMEM] + [HBM] * 11,
        out_specs=(VMEM, HBM, HBM),
        scratch_shapes=[
            pltpu.SMEM((1, blocks), jnp.int32),
            pltpu.SMEM((1, blocks), jnp.int32),
            pltpu.VMEM((tok, width), BF16),
            pltpu.VMEM((tok, kv_width), BF16),
            pltpu.VMEM((tok, kv_width), BF16),
            pltpu.VMEM((rank, cols, tenants), BF16),
            pltpu.VMEM((rank, cols, tenants), BF16),
            pltpu.VMEM((blocks, rank, feat), BF16),
            pltpu.VMEM((blocks, rank, feat), BF16),
            pltpu.VMEM((blocks, rank, LANE), F32),
            pltpu.VMEM((tok, 2 * kv_width), BF16),
            pltpu.VMEM((4 * rank, kv_width), BF16),
            pltpu.SemaphoreType.DMA((7,)),
            pltpu.SemaphoreType.DMA((2, blocks)),
            pltpu.SemaphoreType.DMA((4,)),
        ],
        compiler_params=PARAMS,
        name="pack",
    )(
        me, hbm(tenant_of_block), hbm(live_token_count), hbm(x), hbm(kg), hbm(vg),
        hbm(bk.transpose(1, 2, 0)), hbm(bv.transpose(1, 2, 0)), hbm(ak), hbm(av), hbm(wk), hbm(wv),
    )
    recv = lax.all_to_all(send, ("x", "y"), split_axis=0, concat_axis=0, tiled=True)
    siblings = [(0, 1), (1, 0)]
    other = lax.ppermute(recv, "core", siblings)
    half_vec = pl.pallas_call(
        half_kernel,
        out_shape=jax.ShapeDtypeStruct((tok, LANE), F32),
        in_specs=[SMEM, VMEM, VMEM],
        out_specs=VMEM,
        compiler_params=PARAMS,
        name="half",
    )(me, send, recv)
    vec_send = pl.pallas_call(
        vector_kernel,
        out_shape=jax.ShapeDtypeStruct((n_mp, tok, LANE), F32),
        in_specs=[SMEM, VMEM, VMEM, VMEM],
        out_specs=VMEM,
        compiler_params=PARAMS,
        name="vectors",
    )(me, send, other, half_vec)
    vec = lax.all_to_all(vec_send, mp, split_axis=0, concat_axis=0, tiled=True)
    groups = [jax.ShapeDtypeStruct((blocks * n + blocks, LANE), F32) for n in PIECES]
    top, bottom, low = pl.pallas_call(
        parts_kernel,
        out_shape=(*groups, jax.ShapeDtypeStruct((n_mp // 2, tok, LANE), BF16)),
        in_specs=[SMEM, SMEM, VMEM, VMEM, VMEM],
        out_specs=(VMEM, VMEM, VMEM),
        compiler_params=PARAMS,
        name="parts",
    )(me, tenant_of_block, vec, recv, other)

    dp = ("zh", "zl")
    n_dp = lax.axis_size(dp)
    pairs = [(z, z ^ 1) for z in range(n_dp)]
    others = [(z, (z + (1 if z % 2 else -1)) % n_dp) for z in range(n_dp)]
    got_top = lax.ppermute(top, dp, pairs)
    got_bottom = lax.ppermute(bottom, dp, others)
    plane = lax.axis_index("zl").astype(jnp.int32).reshape(1)
    half = jax.ShapeDtypeStruct((tenants // 2, PART, LANE), F32)
    own = pl.pallas_call(
        own_kernel,
        out_shape=half,
        in_specs=[SMEM, SMEM, VMEM, VMEM],
        out_specs=HBM,
        scratch_shapes=[
            pltpu.VMEM((tenants // 16, PART, LANE), F32),
            pltpu.SemaphoreType.DMA((8,)),
            pltpu.SemaphoreType.DMA((2, blocks)),
        ],
        compiler_params=PARAMS,
        name="own",
    )(plane, tenant_of_block, top, bottom)
    got_top, bundle = lax.optimization_barrier((got_top, bundle))
    far = lax.ppermute(bundle, "core", siblings)
    sums = pl.pallas_call(
        merge_kernel,
        out_shape=half,
        in_specs=[SMEM, SMEM, VMEM, VMEM, VMEM, VMEM, HBM],
        out_specs=HBM,
        scratch_shapes=[
            *[pltpu.VMEM((blocks, n, LANE), F32) for n in PIECES],
            pltpu.SemaphoreType.DMA((2, blocks)),
        ],
        input_output_aliases={6: 0},
        compiler_params=PARAMS,
        name="merge",
    )(plane, tenant_of_block, top, bottom, got_top, got_bottom, own)

    sums, masked = lax.optimization_barrier((sums, masked))
    sums = lax.psum_scatter(sums, "zh", scatter_dimension=0, tiled=True)

    def swap(a, axes):
        return lax.all_to_all(a, axes, split_axis=0, concat_axis=0, tiled=True)

    kv = swap(jnp.broadcast_to(masked[None], (n_mp // 2, *masked.shape)), ("x", "y"))
    w, a = pl.pallas_call(
        weights_kernel,
        out_shape=(
            pltpu.VMEM((2 * feat, 2 * kv_width), BF16),
            jax.ShapeDtypeStruct((blocks, 4 * rank, 2 * feat), BF16),
        ),
        in_specs=[SMEM, VMEM, VMEM],
        out_specs=(VMEM, VMEM),
        compiler_params=PARAMS,
        name="weights",
    )(me, bundle, far)
    grad = pl.pallas_call(
        base_kernel,
        out_shape=jax.ShapeDtypeStruct((n_mp // 2, tok, 2 * feat), BF16),
        in_specs=[VMEM, VMEM, HBM, VMEM],
        out_specs=VMEM,
        scratch_shapes=[pltpu.VMEM(a.shape, BF16), pltpu.SemaphoreType.DMA],
        compiler_params=PARAMS,
        name="base",
    )(kv, w, hbm(a), low)
    grad = swap(grad, ("y", "x"))
    grad_in = grad.transpose(1, 0, 2).reshape(tok, width)
    sums, grad_in = lax.optimization_barrier((sums, grad_in))

    owned = tenants // lax.axis_size(("zh", "zl"))
    grads = pl.pallas_call(
        finish_kernel,
        out_shape=(
            jax.ShapeDtypeStruct((owned, rank, feat), F32),
            jax.ShapeDtypeStruct((owned, rank, feat), F32),
            jax.ShapeDtypeStruct((owned, rank, bk.shape[2]), F32),
            jax.ShapeDtypeStruct((owned, rank, bk.shape[2]), F32),
        ),
        in_specs=[HBM],
        out_specs=(VMEM, VMEM, VMEM, VMEM),
        scratch_shapes=[pltpu.VMEM((owned, PART, LANE), F32), pltpu.SemaphoreType.DMA],
        compiler_params=PARAMS,
        name="finish",
    )(hbm(sums))
    return (grad_in, *grads)


def solution(mesh):
    n_dp, n_mp = mesh.devices.shape
    fine = Mesh(
        mesh.devices.reshape(n_dp // 2, 2, 4, n_mp // 8, 2), ("zh", "zl", "y", "x", "core")
    )
    dp, mp = ("zh", "zl"), ("y", "x", "core")
    rows = P((*dp, *mp), None)
    in_specs = (
        rows, rows, rows,
        P(mp, None), P(mp, None),
        P(None, None, mp), P(None, None, mp), P(None, None, mp), P(None, None, mp),
        P(dp, None), P(dp, None),
    )
    grads = P(dp, None, mp)
    return jax.shard_map(
        shards, mesh=fine, in_specs=in_specs, out_specs=(rows, grads, grads, grads, grads),
        check_vma=False,
    )
```

```python
import functools

import jax
import jax.numpy as jnp
from jax import lax
from jax.experimental import pallas as pl
from jax.experimental.pallas import tpu as pltpu
from jax.sharding import Mesh, PartitionSpec as P

BLOCK = 128
SCALE = 0.5
F32 = jnp.float32
BF16 = jnp.bfloat16
VMEM = pl.BlockSpec(memory_space=pltpu.VMEM)
SMEM = pl.BlockSpec(memory_space=pltpu.SMEM)
HBM = pl.BlockSpec(memory_space=pltpu.HBM)
PARAMS = pltpu.CompilerParams(vmem_limit_bytes=24 * 1024 * 1024)
LANE = 128

PACKED = 224


def slot(chip):
    return chip % 4 * 4 + chip // 4


def tokens_of(ref, chip, core):
    at = pl.multiple_of(96 + 64 * core, 32)
    return ref[slot(chip), pl.ds(at, 32), :], ref[slot(chip), pl.ds(at + 32, 32), :]


def pack_kernel(
    where, tenants_hbm, counts_hbm, x_hbm, k_hbm, v_hbm, bk_hbm, bv_hbm, ak_hbm, av_hbm, wk_hbm, wv_hbm,
    send_ref, masked_hbm, bundle_hbm,
    tenants, counts, x_ref, k_ref, v_ref, bk_ref, bv_ref, ak, av, up, masked, low, sems, a_sems, out_sems,
):
    n_mp = 2 * send_ref.shape[0]
    blocks, rank, feat = ak.shape
    tok, kv_width = k_ref.shape
    cols = kv_width // n_mp
    quad = n_mp // blocks
    pairs = (
        (tenants_hbm, tenants), (counts_hbm, counts), (x_hbm, x_ref), (k_hbm, k_ref),
        (v_hbm, v_ref), (bk_hbm, bk_ref), (bv_hbm, bv_ref),
    )
    loads = [pltpu.make_async_copy(src, dst, sems.at[i]) for i, (src, dst) in enumerate(pairs)]
    for c in loads:
        c.start()
    feat_rows = pl.ds(0, feat), pl.ds(feat, feat)
    stores = [
        pltpu.make_async_copy(wk_hbm, bundle_hbm.at[feat_rows[0]], out_sems.at[0]),
        pltpu.make_async_copy(wv_hbm, bundle_hbm.at[feat_rows[1]], out_sems.at[1]),
        pltpu.make_async_copy(masked, masked_hbm, out_sems.at[2]),
        pltpu.make_async_copy(low, bundle_hbm.at[pl.ds(2 * feat, low.shape[0])], out_sems.at[3]),
    ]
    loads[0].wait()
    copies = []
    for b in range(blocks):
        t = tenants[0, b]
        copies.append(pltpu.make_async_copy(ak_hbm.at[t], ak.at[b], a_sems.at[0, b]))
        copies.append(pltpu.make_async_copy(av_hbm.at[t], av.at[b], a_sems.at[1, b]))
    for c in copies:
        c.start()
    stores[0].start()
    stores[1].start()
    loads[2].wait()
    x = x_ref[...]
    for j in range(n_mp):
        at = 96 + 64 * (j % 2)
        send_ref[slot(j // 2), at : at + 32, :] = x[:, feat * j : feat * j + LANE]
    for i in (1, 3, 4):
        loads[i].wait()
    me = where[0]
    count = counts[0, me // quad]
    row = lax.broadcasted_iota(jnp.int32, (tok, 1), 0) + (me % quad) * tok
    live = row < count
    mk = jnp.where(live, k_ref[...].astype(F32), 0.0).astype(BF16)
    mv = jnp.where(live, v_ref[...].astype(F32), 0.0).astype(BF16)
    masked[:, :kv_width] = mk
    masked[:, kv_width:] = mv
    stores[2].start()
    for j in range(n_mp):
        at = 128 + 64 * (j % 2)
        last = x[:, feat * j + LANE : feat * (j + 1)]
        send_ref[slot(j // 2), at : at + 32, :] = jnp.concatenate(
            [last, mk[:, cols * j : cols * (j + 1)], last, mv[:, cols * j : cols * (j + 1)]], axis=1
        )
    for i in (5, 6):
        loads[i].wait()
    which = lax.broadcasted_iota(jnp.int32, (blocks, bk_ref.shape[2]), 0)
    tenant = jnp.zeros_like(which)
    for b in range(blocks):
        tenant = jnp.where(which == b, tenants[0, b], tenant)
    hot = lax.broadcasted_iota(jnp.int32, tenant.shape, 1) == tenant
    hot = jnp.where(hot, 1.0, 0.0).astype(BF16)
    for ref, at in ((bk_ref, 32), (bv_ref, 96)):
        flat = ref[...].reshape(rank * cols, ref.shape[2])
        got = lax.dot_general(hot, flat, (((1,), (1,)), ((), ())), preferred_element_type=F32)
        for r in range(rank):
            up[:, r, at : at + cols] = got[:, cols * r : cols * (r + 1)]
    for c in copies:
        c.wait()
    for b in range(blocks):
        at = slice(LANE * b, LANE * (b + 1))
        for i, ref in enumerate((ak, av)):
            low[rank * i : rank * (i + 1), at] = ref[b][:, :LANE]
            low[rank * (2 + i) : rank * (3 + i), LANE * b : LANE * b + feat - LANE] = ref[b][:, LANE:]
    stores[3].start()
    for b in range(blocks):
        a0 = ak[b]
        a1 = av[b]
        main = jnp.concatenate([a0[:, :LANE], a1[:, :LANE]], axis=0)
        near = up[b].astype(BF16)
        tail = jnp.concatenate(
            [a0[:, LANE:], near[:, 32:64], a1[:, LANE:], near[:, 96:128]], axis=1
        )
        for q in range(quad // 2):
            send_ref[slot(quad // 2 * b + q), 0:64, :] = main
            send_ref[slot(quad // 2 * b + q), 64:96, :] = tail
    for c in stores:
        c.wait()


def lane_mask(rows, slot):
    lane = lax.broadcasted_iota(jnp.int32, (rows, LANE), 1)
    return (lane >= 32 * slot) & (lane < 32 * slot + 32)


def vectors_of(send_ref, ref, core):
    masks = [lane_mask(32, s) for s in (0, 2, 1, 3)]
    total = jnp.zeros((32, LANE), F32)
    zero = jnp.zeros((64, LANE), BF16)
    for chip in range(send_ref.shape[0]):
        lhs = jnp.concatenate(tokens_of(send_ref, chip, core), axis=1)
        main = jnp.concatenate([ref[slot(chip), 0:64, :], zero], axis=0)
        tail = ref[slot(chip), 64:96, :]
        tails = jnp.concatenate([jnp.where(k, tail, jnp.zeros_like(tail)) for k in masks], axis=0)
        rhs = jnp.concatenate([main, tails], axis=1)
        total += lax.dot_general(lhs, rhs, (((1,), (1,)), ((), ())), preferred_element_type=F32)
    return total


def half_kernel(where, send_ref, recv_ref, out_ref):
    out_ref[...] = vectors_of(send_ref, recv_ref, where[0] % 2)


def vector_kernel(where, send_ref, other_ref, half_ref, out_ref):
    total = half_ref[...] + vectors_of(send_ref, other_ref, 1 - where[0] % 2)
    for m in range(out_ref.shape[0]):
        out_ref[m] = total


def split(x):
    hi = x.astype(BF16)
    return hi, (x - hi.astype(F32)).astype(BF16)


def first_blocks(tenants, blocks):
    first = []
    for b in range(blocks):
        f = jnp.int32(b)
        for c in range(b - 1, -1, -1):
            f = jnp.where(tenants[0, c] == tenants[0, b], c, f)
        first.append(f)
    return first


PIECES = (64, 32)
PART = sum(PIECES)


def block_product(vec_ref, recv_ref, core, b):
    vec, near, far = [], [], []
    for chip in (2 * b, 2 * b + 1):
        vec.append(vec_ref[slot(chip)] * SCALE)
        first_part, last_part = tokens_of(recv_ref, chip, core)
        near.append(first_part)
        far.append(last_part)
    lhs = jnp.concatenate(split(jnp.concatenate(vec, axis=0)), axis=0)
    rhs = jnp.concatenate([jnp.concatenate(near, axis=0), jnp.concatenate(far, axis=0)], axis=1)
    rhs = jnp.concatenate([rhs, rhs], axis=0)
    return lax.dot_general(lhs, rhs, (((0,), (0,)), ((), ())), preferred_element_type=F32)


def half_parts_kernel(where, vec_ref, recv_ref, out_ref, low_ref):
    core = where[0] % 2
    for b in range(out_ref.shape[0]):
        out_ref[b] = block_product(vec_ref, recv_ref, core, b)
    for chip in range(low_ref.shape[0]):
        back = vec_ref[slot(chip)][:, 64:] * SCALE
        low_ref[chip] = jnp.concatenate(split(back), axis=1)


def parts_kernel(where, tenants, vec_ref, recv_ref, half_ref, top_ref, bottom_ref):
    core = where[0] % 2
    blocks = half_ref.shape[0]
    m0, m1, m2, m3 = [lane_mask(32, s) for s in range(4)]
    first = first_blocks(tenants, blocks)
    top_ref[...] = jnp.zeros_like(top_ref)
    bottom_ref[...] = jnp.zeros_like(bottom_ref)
    for b in range(blocks):
        p = half_ref[b] + block_product(vec_ref, recv_ref, core, b)
        q = p[:, LANE:]
        tail = jnp.where(m0, q[64:96], jnp.where(m1, q[0:32], jnp.where(m2, q[96:128], q[32:64])))
        top_ref[pl.ds(pl.multiple_of(first[b] * 64, 8), 64), :] += p[64:128, :LANE]
        bottom_ref[pl.ds(pl.multiple_of(first[b] * 32, 8), 32), :] += tail
    row = lax.broadcasted_iota(jnp.int32, (blocks, LANE), 0)
    ids = jnp.full((blocks, LANE), -1, jnp.int32)
    for b in range(blocks):
        ids = jnp.where((row == b) & (first[b] == b), tenants[0, b], ids)
    top_ref[blocks * 64 :, :] = ids.astype(F32)
    bottom_ref[blocks * 32 :, :] = ids.astype(F32)


def kept(tenant, parity):
    return (tenant >= 0) & ((tenant // 4) % 2 == parity), (tenant // 8) * 4 + tenant % 4


def piece_of(out_hbm, mine, place, h):
    return out_hbm.at[jnp.where(mine, place, 0), pl.ds(sum(PIECES[:h]), PIECES[h])]


def own_kernel(plane, tenants, top_ref, bottom_ref, out_hbm, zeros, fill_sems, sems):
    blocks = sems.shape[1]
    zeros[...] = jnp.zeros_like(zeros)
    chunk = zeros.shape[0]
    fills = [
        pltpu.make_async_copy(zeros, out_hbm.at[pl.ds(i * chunk, chunk)], fill_sems.at[i])
        for i in range(out_hbm.shape[0] // chunk)
    ]
    for c in fills:
        c.start()
    first = first_blocks(tenants, blocks)
    for c in fills:
        c.wait()
    todo = []
    for b in range(blocks):
        mine, place = kept(tenants[0, b], plane[0] % 2)
        mine = mine & (first[b] == b)
        for h, ref in enumerate((top_ref, bottom_ref)):
            src = ref.at[pl.ds(b * PIECES[h], PIECES[h])]
            dst = piece_of(out_hbm, mine, place, h)
            todo.append((mine, pltpu.make_async_copy(src, dst, sems.at[h, b])))
    for mine, copy in todo:
        pl.when(mine)(copy.start)
    for mine, copy in todo:
        pl.when(mine)(copy.wait)


def merge_kernel(
    plane, tenants, top_ref, bottom_ref, got_top, got_bottom, own_hbm, out_hbm,
    top_buf, bottom_buf, sems,
):
    blocks = sems.shape[1]
    gots = got_top, got_bottom
    todo = []
    for h, (ref, got, buf) in enumerate(zip((top_ref, bottom_ref), gots, (top_buf, bottom_buf))):
        size = PIECES[h]
        for b in range(blocks):
            tenant = got[blocks * size + b, 0].astype(jnp.int32)
            mine, place = kept(tenant, plane[0] % 2)
            same = jnp.int32(-1)
            for c in range(blocks - 1, -1, -1):
                same = jnp.where(tenants[0, c] == tenant, c, same)
            at = pl.multiple_of(jnp.maximum(same, 0) * size, 8)
            here = jnp.where(same >= 0, 1.0, 0.0)
            buf[b] = got[b * size : (b + 1) * size, :] + ref[pl.ds(at, size), :] * here
            copy = pltpu.make_async_copy(buf.at[b], piece_of(out_hbm, mine, place, h), sems.at[h, b])
            pl.when(mine)(copy.start)
            todo.append((mine, copy))
    for mine, copy in todo:
        pl.when(mine)(copy.wait)


def weights_kernel(where, near_ref, far_ref, w_ref, a_ref):
    width = near_ref.shape[1]
    blocks = a_ref.shape[0]
    feat = w_ref.shape[0] // 2
    rank = a_ref.shape[1] // 4
    core = where[0] % 2
    for c, ref in enumerate((near_ref, far_ref)):
        at = pl.multiple_of(jnp.where(core == 0, c, 1 - c) * feat, 16)
        w_ref[pl.ds(at, feat), :width] = ref[0:feat, :]
        w_ref[pl.ds(at, feat), width:] = ref[feat : 2 * feat, :]
    first = 2 * feat
    for b in range(blocks):
        pair = []
        for ref in (near_ref, far_ref):
            main = ref[first : first + 2 * rank, LANE * b : LANE * (b + 1)]
            rest = ref[first + 2 * rank :, LANE * b : LANE * b + feat - LANE]
            pair.append(jnp.concatenate([main, rest], axis=1).astype(F32))
        same, other = jnp.concatenate(pair, axis=1), jnp.concatenate(pair[::-1], axis=1)
        a = jnp.where(core == 0, same, other).astype(BF16)
        a_ref[b, : 2 * rank, :] = a
        a_ref[b, 2 * rank :, :] = a


def base_kernel(kv_ref, w_ref, a_hbm, low_ref, out_ref, a_ref, sem):
    load = pltpu.make_async_copy(a_hbm, a_ref, sem)
    load.start()
    blocks = a_ref.shape[0]
    per = kv_ref.shape[0] // blocks
    step = 4
    for s in range(0, blocks, step):
        rows = [kv_ref[i % 4 * (kv_ref.shape[0] // 4) + i // 4] for i in range(per * s, per * (s + step))]
        rows = jnp.concatenate(rows, axis=0)
        res = lax.dot_general(rows, w_ref[...], (((1,), (1,)), ((), ())), preferred_element_type=F32)
        size = res.shape[0] // step
        if s == 0:
            load.wait()
        for i in range(step):
            b = s + i
            low = low_ref[per * b : per * (b + 1)].reshape(-1, LANE)
            total = res[size * i : size * (i + 1)] + jnp.dot(low, a_ref[b], preferred_element_type=F32)
            out_ref[per * b : per * (b + 1)] = total.astype(BF16).reshape(per, -1, w_ref.shape[0])


def finish_kernel(sum_hbm, ak_ref, av_ref, bk_ref, bv_ref, sum_ref, sem):
    load = pltpu.make_async_copy(sum_hbm, sum_ref, sem)
    load.start()
    load.wait()
    for t in range(sum_ref.shape[0]):
        tail = sum_ref[t, 64:96, :]
        ak_ref[t, :, :LANE] = sum_ref[t, 0:32, :]
        ak_ref[t, :, LANE:] = tail[:, 0:32]
        av_ref[t, :, :LANE] = sum_ref[t, 32:64, :]
        av_ref[t, :, LANE:] = tail[:, 64:96]
        bk_ref[t] = tail[:, 32:64]
        bv_ref[t] = tail[:, 96:128]


def shards(x, kg, vg, wk, wv, ak, av, bk, bv, tenant_of_block, live_token_count):
    mp = ("y", "x", "core")
    n_mp = lax.axis_size(mp)
    tok, width = x.shape
    blocks = tenant_of_block.shape[1]
    feat = wk.shape[0]
    kv_width = kg.shape[1]
    tenants, rank = ak.shape[:2]
    me = lax.axis_index(mp).astype(jnp.int32).reshape(1)
    cols = bk.shape[2]
    hbm = lambda a: pltpu.with_memory_space_constraint(a, pltpu.HBM)
    bundle_rows = 2 * feat + 4 * rank
    send, masked, bundle = pl.pallas_call(
        pack_kernel,
        out_shape=(
            jax.ShapeDtypeStruct((n_mp // 2, PACKED, LANE), BF16),
            jax.ShapeDtypeStruct((tok, 2 * kv_width), BF16),
            jax.ShapeDtypeStruct((bundle_rows, kv_width), BF16),
        ),
        in_specs=[SMEM] + [HBM] * 11,
        out_specs=(VMEM, HBM, HBM),
        scratch_shapes=[
            pltpu.SMEM((1, blocks), jnp.int32),
            pltpu.SMEM((1, blocks), jnp.int32),
            pltpu.VMEM((tok, width), BF16),
            pltpu.VMEM((tok, kv_width), BF16),
            pltpu.VMEM((tok, kv_width), BF16),
            pltpu.VMEM((rank, cols, tenants), BF16),
            pltpu.VMEM((rank, cols, tenants), BF16),
            pltpu.VMEM((blocks, rank, feat), BF16),
            pltpu.VMEM((blocks, rank, feat), BF16),
            pltpu.VMEM((blocks, rank, LANE), F32),
            pltpu.VMEM((tok, 2 * kv_width), BF16),
            pltpu.VMEM((4 * rank, kv_width), BF16),
            pltpu.SemaphoreType.DMA((7,)),
            pltpu.SemaphoreType.DMA((2, blocks)),
            pltpu.SemaphoreType.DMA((4,)),
        ],
        compiler_params=PARAMS,
        name="pack",
    )(
        me, hbm(tenant_of_block), hbm(live_token_count), hbm(x), hbm(kg), hbm(vg),
        hbm(bk.transpose(1, 2, 0)), hbm(bv.transpose(1, 2, 0)), hbm(ak), hbm(av), hbm(wk), hbm(wv),
    )
    recv = lax.all_to_all(send, ("x", "y"), split_axis=0, concat_axis=0, tiled=True)
    siblings = [(0, 1), (1, 0)]
    other = lax.ppermute(recv, "core", siblings)
    half_vec = pl.pallas_call(
        half_kernel,
        out_shape=jax.ShapeDtypeStruct((tok, LANE), F32),
        in_specs=[SMEM, VMEM, VMEM],
        out_specs=VMEM,
        compiler_params=PARAMS,
        name="half",
    )(me, send, recv)
    vec_send = pl.pallas_call(
        vector_kernel,
        out_shape=jax.ShapeDtypeStruct((n_mp // 2, tok, LANE), F32),
        in_specs=[SMEM, VMEM, VMEM, VMEM],
        out_specs=VMEM,
        compiler_params=PARAMS,
        name="vectors",
    )(me, send, other, half_vec)
    vec = lax.all_to_all(vec_send, ("x", "y"), split_axis=0, concat_axis=0, tiled=True)
    other_vec = lax.ppermute(vec, "core", siblings)
    half_parts, low = pl.pallas_call(
        half_parts_kernel,
        out_shape=(
            jax.ShapeDtypeStruct((blocks, LANE, 2 * LANE), F32),
            jax.ShapeDtypeStruct((n_mp // 2, tok, LANE), BF16),
        ),
        in_specs=[SMEM, VMEM, VMEM],
        out_specs=(VMEM, VMEM),
        compiler_params=PARAMS,
        name="half_parts",
    )(me, vec, recv)
    groups = [jax.ShapeDtypeStruct((blocks * n + blocks, LANE), F32) for n in PIECES]
    top, bottom = pl.pallas_call(
        parts_kernel,
        out_shape=tuple(groups),
        in_specs=[SMEM, SMEM, VMEM, VMEM, VMEM],
        out_specs=(VMEM, VMEM),
        compiler_params=PARAMS,
        name="parts",
    )(me, tenant_of_block, other_vec, other, half_parts)

    dp = ("zh", "zl")
    n_dp = lax.axis_size(dp)
    pairs = [(z, z ^ 1) for z in range(n_dp)]
    others = [(z, (z + (1 if z % 2 else -1)) % n_dp) for z in range(n_dp)]
    got_top = lax.ppermute(top, dp, pairs)
    got_bottom = lax.ppermute(bottom, dp, others)
    plane = lax.axis_index("zl").astype(jnp.int32).reshape(1)
    half = jax.ShapeDtypeStruct((tenants // 2, PART, LANE), F32)
    own = pl.pallas_call(
        own_kernel,
        out_shape=half,
        in_specs=[SMEM, SMEM, VMEM, VMEM],
        out_specs=HBM,
        scratch_shapes=[
            pltpu.VMEM((tenants // 16, PART, LANE), F32),
            pltpu.SemaphoreType.DMA((8,)),
            pltpu.SemaphoreType.DMA((2, blocks)),
        ],
        compiler_params=PARAMS,
        name="own",
    )(plane, tenant_of_block, top, bottom)
    got_top, bundle = lax.optimization_barrier((got_top, bundle))
    far = lax.ppermute(bundle, "core", siblings)
    sums = pl.pallas_call(
        merge_kernel,
        out_shape=half,
        in_specs=[SMEM, SMEM, VMEM, VMEM, VMEM, VMEM, HBM],
        out_specs=HBM,
        scratch_shapes=[
            *[pltpu.VMEM((blocks, n, LANE), F32) for n in PIECES],
            pltpu.SemaphoreType.DMA((2, blocks)),
        ],
        input_output_aliases={6: 0},
        compiler_params=PARAMS,
        name="merge",
    )(plane, tenant_of_block, top, bottom, got_top, got_bottom, own)

    sums, masked = lax.optimization_barrier((sums, masked))
    sums = lax.psum_scatter(sums, "zh", scatter_dimension=0, tiled=True)

    def swap(a, axes):
        return lax.all_to_all(a, axes, split_axis=0, concat_axis=0, tiled=True)

    kv = swap(jnp.broadcast_to(masked[None], (n_mp // 2, *masked.shape)), ("x", "y"))
    w, a = pl.pallas_call(
        weights_kernel,
        out_shape=(
            pltpu.VMEM((2 * feat, 2 * kv_width), BF16),
            jax.ShapeDtypeStruct((blocks, 4 * rank, 2 * feat), BF16),
        ),
        in_specs=[SMEM, VMEM, VMEM],
        out_specs=(VMEM, VMEM),
        compiler_params=PARAMS,
        name="weights",
    )(me, bundle, far)
    grad = pl.pallas_call(
        base_kernel,
        out_shape=jax.ShapeDtypeStruct((n_mp // 2, tok, 2 * feat), BF16),
        in_specs=[VMEM, VMEM, HBM, VMEM],
        out_specs=VMEM,
        scratch_shapes=[pltpu.VMEM(a.shape, BF16), pltpu.SemaphoreType.DMA],
        compiler_params=PARAMS,
        name="base",
    )(kv, w, hbm(a), low)
    grad = swap(grad, ("y", "x"))
    grad_in = grad.transpose(1, 0, 2).reshape(tok, width)
    sums, grad_in = lax.optimization_barrier((sums, grad_in))

    owned = tenants // lax.axis_size(("zh", "zl"))
    grads = pl.pallas_call(
        finish_kernel,
        out_shape=(
            jax.ShapeDtypeStruct((owned, rank, feat), F32),
            jax.ShapeDtypeStruct((owned, rank, feat), F32),
            jax.ShapeDtypeStruct((owned, rank, bk.shape[2]), F32),
            jax.ShapeDtypeStruct((owned, rank, bk.shape[2]), F32),
        ),
        in_specs=[HBM],
        out_specs=(VMEM, VMEM, VMEM, VMEM),
        scratch_shapes=[pltpu.VMEM((owned, PART, LANE), F32), pltpu.SemaphoreType.DMA],
        compiler_params=PARAMS,
        name="finish",
    )(hbm(sums))
    return (grad_in, *grads)


def solution(mesh):
    n_dp, n_mp = mesh.devices.shape
    fine = Mesh(
        mesh.devices.reshape(n_dp // 2, 2, 4, n_mp // 8, 2), ("zh", "zl", "y", "x", "core")
    )
    dp, mp = ("zh", "zl"), ("y", "x", "core")
    rows = P((*dp, *mp), None)
    in_specs = (
        rows, rows, rows,
        P(mp, None), P(mp, None),
        P(None, None, mp), P(None, None, mp), P(None, None, mp), P(None, None, mp),
        P(dp, None), P(dp, None),
    )
    grads = P(dp, None, mp)
    return jax.shard_map(
        shards, mesh=fine, in_specs=in_specs, out_specs=(rows, grads, grads, grads, grads),
        check_vma=False,
    )
```

```python
import functools

import jax
import jax.numpy as jnp
from jax import lax
from jax.experimental import pallas as pl
from jax.experimental.pallas import tpu as pltpu
from jax.sharding import Mesh, PartitionSpec as P

BLOCK = 128
SCALE = 0.5
F32 = jnp.float32
BF16 = jnp.bfloat16
VMEM = pl.BlockSpec(memory_space=pltpu.VMEM)
SMEM = pl.BlockSpec(memory_space=pltpu.SMEM)
HBM = pl.BlockSpec(memory_space=pltpu.HBM)
PARAMS = pltpu.CompilerParams(vmem_limit_bytes=24 * 1024 * 1024)
LANE = 128

PACKED = 224


def slot(chip):
    return chip % 4 * 4 + chip // 4


def tokens_of(ref, chip, core):
    at = pl.multiple_of(96 + 64 * core, 32)
    return ref[slot(chip), pl.ds(at, 32), :], ref[slot(chip), pl.ds(at + 32, 32), :]


def pack_kernel(
    where, tenants_hbm, counts_hbm, x_hbm, k_hbm, v_hbm, bk_hbm, bv_hbm, ak_hbm, av_hbm, wk_hbm, wv_hbm,
    send_ref, masked_hbm, bundle_hbm,
    tenants, counts, x_ref, k_ref, v_ref, bk_ref, bv_ref, ak, av, up, masked, low, sems, a_sems, out_sems,
):
    n_mp = 2 * send_ref.shape[0]
    blocks, rank, feat = ak.shape
    tok, kv_width = k_ref.shape
    cols = kv_width // n_mp
    quad = n_mp // blocks
    pairs = (
        (tenants_hbm, tenants), (counts_hbm, counts), (x_hbm, x_ref), (k_hbm, k_ref),
        (v_hbm, v_ref), (bk_hbm, bk_ref), (bv_hbm, bv_ref),
    )
    loads = [pltpu.make_async_copy(src, dst, sems.at[i]) for i, (src, dst) in enumerate(pairs)]
    for c in loads:
        c.start()
    feat_rows = pl.ds(0, feat), pl.ds(feat, feat)
    stores = [
        pltpu.make_async_copy(wk_hbm, bundle_hbm.at[feat_rows[0]], out_sems.at[0]),
        pltpu.make_async_copy(wv_hbm, bundle_hbm.at[feat_rows[1]], out_sems.at[1]),
        pltpu.make_async_copy(masked, masked_hbm, out_sems.at[2]),
        pltpu.make_async_copy(low, bundle_hbm.at[pl.ds(2 * feat, low.shape[0])], out_sems.at[3]),
    ]
    loads[0].wait()
    copies = []
    for b in range(blocks):
        t = tenants[0, b]
        copies.append(pltpu.make_async_copy(ak_hbm.at[t], ak.at[b], a_sems.at[0, b]))
        copies.append(pltpu.make_async_copy(av_hbm.at[t], av.at[b], a_sems.at[1, b]))
    for c in copies:
        c.start()
    stores[0].start()
    stores[1].start()
    loads[2].wait()
    x = x_ref[...]
    for j in range(n_mp):
        at = 96 + 64 * (j % 2)
        send_ref[slot(j // 2), at : at + 32, :] = x[:, feat * j : feat * j + LANE]
    for i in (1, 3, 4):
        loads[i].wait()
    me = where[0]
    count = counts[0, me // quad]
    row = lax.broadcasted_iota(jnp.int32, (tok, 1), 0) + (me % quad) * tok
    live = row < count
    mk = jnp.where(live, k_ref[...].astype(F32), 0.0).astype(BF16)
    mv = jnp.where(live, v_ref[...].astype(F32), 0.0).astype(BF16)
    masked[:, :kv_width] = mk
    masked[:, kv_width:] = mv
    stores[2].start()
    for j in range(n_mp):
        at = 128 + 64 * (j % 2)
        last = x[:, feat * j + LANE : feat * (j + 1)]
        send_ref[slot(j // 2), at : at + 32, :] = jnp.concatenate(
            [last, mk[:, cols * j : cols * (j + 1)], last, mv[:, cols * j : cols * (j + 1)]], axis=1
        )
    for i in (5, 6):
        loads[i].wait()
    which = lax.broadcasted_iota(jnp.int32, (blocks, bk_ref.shape[2]), 0)
    tenant = jnp.zeros_like(which)
    for b in range(blocks):
        tenant = jnp.where(which == b, tenants[0, b], tenant)
    hot = lax.broadcasted_iota(jnp.int32, tenant.shape, 1) == tenant
    hot = jnp.where(hot, 1.0, 0.0).astype(BF16)
    for ref, at in ((bk_ref, 32), (bv_ref, 96)):
        flat = ref[...].reshape(rank * cols, ref.shape[2])
        got = lax.dot_general(hot, flat, (((1,), (1,)), ((), ())), preferred_element_type=F32)
        for r in range(rank):
            up[:, r, at : at + cols] = got[:, cols * r : cols * (r + 1)]
    for c in copies:
        c.wait()
    for b in range(blocks):
        at = slice(LANE * b, LANE * (b + 1))
        for i, ref in enumerate((ak, av)):
            low[rank * i : rank * (i + 1), at] = ref[b][:, :LANE]
            low[rank * (2 + i) : rank * (3 + i), LANE * b : LANE * b + feat - LANE] = ref[b][:, LANE:]
    stores[3].start()
    for b in range(blocks):
        a0 = ak[b]
        a1 = av[b]
        main = jnp.concatenate([a0[:, :LANE], a1[:, :LANE]], axis=0)
        near = up[b].astype(BF16)
        tail = jnp.concatenate(
            [a0[:, LANE:], near[:, 32:64], a1[:, LANE:], near[:, 96:128]], axis=1
        )
        for q in range(quad // 2):
            send_ref[slot(quad // 2 * b + q), 0:64, :] = main
            send_ref[slot(quad // 2 * b + q), 64:96, :] = tail
    for c in stores:
        c.wait()


def lane_mask(rows, slot):
    lane = lax.broadcasted_iota(jnp.int32, (rows, LANE), 1)
    return (lane >= 32 * slot) & (lane < 32 * slot + 32)


def vectors_of(send_ref, ref, core):
    masks = [lane_mask(32, s) for s in (0, 2, 1, 3)]
    total = jnp.zeros((32, LANE), F32)
    zero = jnp.zeros((64, LANE), BF16)
    for chip in range(send_ref.shape[0]):
        lhs = jnp.concatenate(tokens_of(send_ref, chip, core), axis=1)
        main = jnp.concatenate([ref[slot(chip), 0:64, :], zero], axis=0)
        tail = ref[slot(chip), 64:96, :]
        tails = jnp.concatenate([jnp.where(k, tail, jnp.zeros_like(tail)) for k in masks], axis=0)
        rhs = jnp.concatenate([main, tails], axis=1)
        total += lax.dot_general(lhs, rhs, (((1,), (1,)), ((), ())), preferred_element_type=F32)
    return total


def half_kernel(where, send_ref, recv_ref, out_ref):
    out_ref[...] = vectors_of(send_ref, recv_ref, where[0] % 2)


def vector_kernel(where, send_ref, other_ref, half_ref, out_ref):
    total = half_ref[...] + vectors_of(send_ref, other_ref, 1 - where[0] % 2)
    for m in range(out_ref.shape[0]):
        out_ref[m] = total


def split(x):
    hi = x.astype(BF16)
    return hi, (x - hi.astype(F32)).astype(BF16)


def first_blocks(tenants, blocks):
    first = []
    for b in range(blocks):
        f = jnp.int32(b)
        for c in range(b - 1, -1, -1):
            f = jnp.where(tenants[0, c] == tenants[0, b], c, f)
        first.append(f)
    return first


PIECES = (64, 32)
PART = sum(PIECES)


def block_product(vec_ref, recv_ref, core, b):
    vec, near, far = [], [], []
    for chip in (2 * b, 2 * b + 1):
        vec.append(vec_ref[slot(chip)] * SCALE)
        first_part, last_part = tokens_of(recv_ref, chip, core)
        near.append(first_part)
        far.append(last_part)
    lhs = jnp.concatenate(split(jnp.concatenate(vec, axis=0)), axis=0)
    rhs = jnp.concatenate([jnp.concatenate(near, axis=0), jnp.concatenate(far, axis=0)], axis=1)
    rhs = jnp.concatenate([rhs, rhs], axis=0)
    p = lax.dot_general(lhs, rhs, (((0,), (0,)), ((), ())), preferred_element_type=F32)
    m0, m1, m2, _ = [lane_mask(32, s) for s in range(4)]
    q = p[:, LANE:]
    tail = jnp.where(m0, q[64:96], jnp.where(m1, q[0:32], jnp.where(m2, q[96:128], q[32:64])))
    return p[64:128, :LANE], tail


def half_parts_kernel(where, vec_ref, recv_ref, out_ref, low_ref):
    core = where[0] % 2
    for b in range(out_ref.shape[0]):
        main, tail = block_product(vec_ref, recv_ref, core, b)
        out_ref[b, 0:64, :] = main
        out_ref[b, 64:96, :] = tail
    for chip in range(low_ref.shape[0]):
        back = vec_ref[slot(chip)][:, 64:] * SCALE
        low_ref[chip] = jnp.concatenate(split(back), axis=1)


def parts_kernel(where, tenants, vec_ref, recv_ref, half_ref, top_ref, bottom_ref):
    core = where[0] % 2
    blocks = half_ref.shape[0]
    first = first_blocks(tenants, blocks)
    top_ref[...] = jnp.zeros_like(top_ref)
    bottom_ref[...] = jnp.zeros_like(bottom_ref)
    for b in range(blocks):
        main, tail = block_product(vec_ref, recv_ref, core, b)
        top_ref[pl.ds(pl.multiple_of(first[b] * 64, 8), 64), :] += half_ref[b, 0:64, :] + main
        bottom_ref[pl.ds(pl.multiple_of(first[b] * 32, 8), 32), :] += half_ref[b, 64:96, :] + tail
    row = lax.broadcasted_iota(jnp.int32, (blocks, LANE), 0)
    ids = jnp.full((blocks, LANE), -1, jnp.int32)
    for b in range(blocks):
        ids = jnp.where((row == b) & (first[b] == b), tenants[0, b], ids)
    top_ref[blocks * 64 :, :] = ids.astype(F32)
    bottom_ref[blocks * 32 :, :] = ids.astype(F32)


def kept(tenant, parity):
    return (tenant >= 0) & ((tenant // 4) % 2 == parity), (tenant // 8) * 4 + tenant % 4


def piece_of(out_hbm, mine, place, h):
    return out_hbm.at[jnp.where(mine, place, 0), pl.ds(sum(PIECES[:h]), PIECES[h])]


def own_kernel(plane, tenants, top_ref, bottom_ref, out_hbm, zeros, fill_sems, sems):
    blocks = sems.shape[1]
    zeros[...] = jnp.zeros_like(zeros)
    chunk = zeros.shape[0]
    fills = [
        pltpu.make_async_copy(zeros, out_hbm.at[pl.ds(i * chunk, chunk)], fill_sems.at[i])
        for i in range(out_hbm.shape[0] // chunk)
    ]
    for c in fills:
        c.start()
    first = first_blocks(tenants, blocks)
    for c in fills:
        c.wait()
    todo = []
    for b in range(blocks):
        mine, place = kept(tenants[0, b], plane[0] % 2)
        mine = mine & (first[b] == b)
        for h, ref in enumerate((top_ref, bottom_ref)):
            src = ref.at[pl.ds(b * PIECES[h], PIECES[h])]
            dst = piece_of(out_hbm, mine, place, h)
            todo.append((mine, pltpu.make_async_copy(src, dst, sems.at[h, b])))
    for mine, copy in todo:
        pl.when(mine)(copy.start)
    for mine, copy in todo:
        pl.when(mine)(copy.wait)


def merge_kernel(
    plane, tenants, top_ref, bottom_ref, got_top, got_bottom, own_hbm, out_hbm,
    top_buf, bottom_buf, sems,
):
    blocks = sems.shape[1]
    gots = got_top, got_bottom
    todo = []
    for h, (ref, got, buf) in enumerate(zip((top_ref, bottom_ref), gots, (top_buf, bottom_buf))):
        size = PIECES[h]
        for b in range(blocks):
            tenant = got[blocks * size + b, 0].astype(jnp.int32)
            mine, place = kept(tenant, plane[0] % 2)
            same = jnp.int32(-1)
            for c in range(blocks - 1, -1, -1):
                same = jnp.where(tenants[0, c] == tenant, c, same)
            at = pl.multiple_of(jnp.maximum(same, 0) * size, 8)
            here = jnp.where(same >= 0, 1.0, 0.0)
            buf[b] = got[b * size : (b + 1) * size, :] + ref[pl.ds(at, size), :] * here
            copy = pltpu.make_async_copy(buf.at[b], piece_of(out_hbm, mine, place, h), sems.at[h, b])
            pl.when(mine)(copy.start)
            todo.append((mine, copy))
    for mine, copy in todo:
        pl.when(mine)(copy.wait)


def weights_kernel(where, near_ref, far_ref, w_ref, a_ref):
    width = near_ref.shape[1]
    blocks = a_ref.shape[0]
    feat = w_ref.shape[0] // 2
    rank = a_ref.shape[1] // 4
    core = where[0] % 2
    for c, ref in enumerate((near_ref, far_ref)):
        at = pl.multiple_of(jnp.where(core == 0, c, 1 - c) * feat, 16)
        w_ref[pl.ds(at, feat), :width] = ref[0:feat, :]
        w_ref[pl.ds(at, feat), width:] = ref[feat : 2 * feat, :]
    first = 2 * feat
    for b in range(blocks):
        pair = []
        for ref in (near_ref, far_ref):
            main = ref[first : first + 2 * rank, LANE * b : LANE * (b + 1)]
            rest = ref[first + 2 * rank :, LANE * b : LANE * b + feat - LANE]
            pair.append(jnp.concatenate([main, rest], axis=1).astype(F32))
        same, other = jnp.concatenate(pair, axis=1), jnp.concatenate(pair[::-1], axis=1)
        a = jnp.where(core == 0, same, other).astype(BF16)
        a_ref[b, : 2 * rank, :] = a
        a_ref[b, 2 * rank :, :] = a


def base_kernel(kv_ref, w_ref, a_hbm, low_ref, out_ref, a_ref, sem):
    load = pltpu.make_async_copy(a_hbm, a_ref, sem)
    load.start()
    blocks = a_ref.shape[0]
    per = kv_ref.shape[0] // blocks
    step = 4
    for s in range(0, blocks, step):
        rows = [kv_ref[i % 4 * (kv_ref.shape[0] // 4) + i // 4] for i in range(per * s, per * (s + step))]
        rows = jnp.concatenate(rows, axis=0)
        res = lax.dot_general(rows, w_ref[...], (((1,), (1,)), ((), ())), preferred_element_type=F32)
        size = res.shape[0] // step
        if s == 0:
            load.wait()
        for i in range(step):
            b = s + i
            low = low_ref[per * b : per * (b + 1)].reshape(-1, LANE)
            total = res[size * i : size * (i + 1)] + jnp.dot(low, a_ref[b], preferred_element_type=F32)
            out_ref[per * b : per * (b + 1)] = total.astype(BF16).reshape(per, -1, w_ref.shape[0])


def finish_kernel(sum_hbm, ak_ref, av_ref, bk_ref, bv_ref, sum_ref, sem):
    load = pltpu.make_async_copy(sum_hbm, sum_ref, sem)
    load.start()
    load.wait()
    for t in range(sum_ref.shape[0]):
        tail = sum_ref[t, 64:96, :]
        ak_ref[t, :, :LANE] = sum_ref[t, 0:32, :]
        ak_ref[t, :, LANE:] = tail[:, 0:32]
        av_ref[t, :, :LANE] = sum_ref[t, 32:64, :]
        av_ref[t, :, LANE:] = tail[:, 64:96]
        bk_ref[t] = tail[:, 32:64]
        bv_ref[t] = tail[:, 96:128]


def shards(x, kg, vg, wk, wv, ak, av, bk, bv, tenant_of_block, live_token_count):
    mp = ("y", "x", "core")
    n_mp = lax.axis_size(mp)
    tok, width = x.shape
    blocks = tenant_of_block.shape[1]
    feat = wk.shape[0]
    kv_width = kg.shape[1]
    tenants, rank = ak.shape[:2]
    me = lax.axis_index(mp).astype(jnp.int32).reshape(1)
    cols = bk.shape[2]
    hbm = lambda a: pltpu.with_memory_space_constraint(a, pltpu.HBM)
    bundle_rows = 2 * feat + 4 * rank
    send, masked, bundle = pl.pallas_call(
        pack_kernel,
        out_shape=(
            jax.ShapeDtypeStruct((n_mp // 2, PACKED, LANE), BF16),
            jax.ShapeDtypeStruct((tok, 2 * kv_width), BF16),
            jax.ShapeDtypeStruct((bundle_rows, kv_width), BF16),
        ),
        in_specs=[SMEM] + [HBM] * 11,
        out_specs=(VMEM, HBM, HBM),
        scratch_shapes=[
            pltpu.SMEM((1, blocks), jnp.int32),
            pltpu.SMEM((1, blocks), jnp.int32),
            pltpu.VMEM((tok, width), BF16),
            pltpu.VMEM((tok, kv_width), BF16),
            pltpu.VMEM((tok, kv_width), BF16),
            pltpu.VMEM((rank, cols, tenants), BF16),
            pltpu.VMEM((rank, cols, tenants), BF16),
            pltpu.VMEM((blocks, rank, feat), BF16),
            pltpu.VMEM((blocks, rank, feat), BF16),
            pltpu.VMEM((blocks, rank, LANE), F32),
            pltpu.VMEM((tok, 2 * kv_width), BF16),
            pltpu.VMEM((4 * rank, kv_width), BF16),
            pltpu.SemaphoreType.DMA((7,)),
            pltpu.SemaphoreType.DMA((2, blocks)),
            pltpu.SemaphoreType.DMA((4,)),
        ],
        compiler_params=PARAMS,
        name="pack",
    )(
        me, hbm(tenant_of_block), hbm(live_token_count), hbm(x), hbm(kg), hbm(vg),
        hbm(bk.transpose(1, 2, 0)), hbm(bv.transpose(1, 2, 0)), hbm(ak), hbm(av), hbm(wk), hbm(wv),
    )
    recv = lax.all_to_all(send, ("x", "y"), split_axis=0, concat_axis=0, tiled=True)
    siblings = [(0, 1), (1, 0)]
    other = lax.ppermute(recv, "core", siblings)
    half_vec = pl.pallas_call(
        half_kernel,
        out_shape=jax.ShapeDtypeStruct((tok, LANE), F32),
        in_specs=[SMEM, VMEM, VMEM],
        out_specs=VMEM,
        compiler_params=PARAMS,
        name="half",
    )(me, send, recv)
    vec_send = pl.pallas_call(
        vector_kernel,
        out_shape=jax.ShapeDtypeStruct((n_mp // 2, tok, LANE), F32),
        in_specs=[SMEM, VMEM, VMEM, VMEM],
        out_specs=VMEM,
        compiler_params=PARAMS,
        name="vectors",
    )(me, send, other, half_vec)
    vec = lax.all_to_all(vec_send, ("x", "y"), split_axis=0, concat_axis=0, tiled=True)
    other_vec = lax.ppermute(vec, "core", siblings)
    half_parts, low = pl.pallas_call(
        half_parts_kernel,
        out_shape=(
            jax.ShapeDtypeStruct((blocks, PART, LANE), F32),
            jax.ShapeDtypeStruct((n_mp // 2, tok, LANE), BF16),
        ),
        in_specs=[SMEM, VMEM, VMEM],
        out_specs=(VMEM, VMEM),
        compiler_params=PARAMS,
        name="half_parts",
    )(me, vec, recv)
    groups = [jax.ShapeDtypeStruct((blocks * n + blocks, LANE), F32) for n in PIECES]
    top, bottom = pl.pallas_call(
        parts_kernel,
        out_shape=tuple(groups),
        in_specs=[SMEM, SMEM, VMEM, VMEM, VMEM],
        out_specs=(VMEM, VMEM),
        compiler_params=PARAMS,
        name="parts",
    )(me, tenant_of_block, other_vec, other, half_parts)

    dp = ("zh", "zl")
    n_dp = lax.axis_size(dp)
    pairs = [(z, z ^ 1) for z in range(n_dp)]
    others = [(z, (z + (1 if z % 2 else -1)) % n_dp) for z in range(n_dp)]
    got_top = lax.ppermute(top, dp, pairs)
    got_bottom = lax.ppermute(bottom, dp, others)
    plane = lax.axis_index("zl").astype(jnp.int32).reshape(1)
    half = jax.ShapeDtypeStruct((tenants // 2, PART, LANE), F32)
    own = pl.pallas_call(
        own_kernel,
        out_shape=half,
        in_specs=[SMEM, SMEM, VMEM, VMEM],
        out_specs=HBM,
        scratch_shapes=[
            pltpu.VMEM((tenants // 16, PART, LANE), F32),
            pltpu.SemaphoreType.DMA((8,)),
            pltpu.SemaphoreType.DMA((2, blocks)),
        ],
        compiler_params=PARAMS,
        name="own",
    )(plane, tenant_of_block, top, bottom)
    got_top, bundle = lax.optimization_barrier((got_top, bundle))
    far = lax.ppermute(bundle, "core", siblings)
    sums = pl.pallas_call(
        merge_kernel,
        out_shape=half,
        in_specs=[SMEM, SMEM, VMEM, VMEM, VMEM, VMEM, HBM],
        out_specs=HBM,
        scratch_shapes=[
            *[pltpu.VMEM((blocks, n, LANE), F32) for n in PIECES],
            pltpu.SemaphoreType.DMA((2, blocks)),
        ],
        input_output_aliases={6: 0},
        compiler_params=PARAMS,
        name="merge",
    )(plane, tenant_of_block, top, bottom, got_top, got_bottom, own)

    sums, masked = lax.optimization_barrier((sums, masked))
    sums = lax.psum_scatter(sums, "zh", scatter_dimension=0, tiled=True)

    def swap(a, axes):
        return lax.all_to_all(a, axes, split_axis=0, concat_axis=0, tiled=True)

    kv = swap(jnp.broadcast_to(masked[None], (n_mp // 2, *masked.shape)), ("x", "y"))
    w, a = pl.pallas_call(
        weights_kernel,
        out_shape=(
            pltpu.VMEM((2 * feat, 2 * kv_width), BF16),
            jax.ShapeDtypeStruct((blocks, 4 * rank, 2 * feat), BF16),
        ),
        in_specs=[SMEM, VMEM, VMEM],
        out_specs=(VMEM, VMEM),
        compiler_params=PARAMS,
        name="weights",
    )(me, bundle, far)
    grad = pl.pallas_call(
        base_kernel,
        out_shape=jax.ShapeDtypeStruct((n_mp // 2, tok, 2 * feat), BF16),
        in_specs=[VMEM, VMEM, HBM, VMEM],
        out_specs=VMEM,
        scratch_shapes=[pltpu.VMEM(a.shape, BF16), pltpu.SemaphoreType.DMA],
        compiler_params=PARAMS,
        name="base",
    )(kv, w, hbm(a), low)
    grad = swap(grad, ("y", "x"))
    grad_in = grad.transpose(1, 0, 2).reshape(tok, width)
    sums, grad_in = lax.optimization_barrier((sums, grad_in))

    owned = tenants // lax.axis_size(("zh", "zl"))
    grads = pl.pallas_call(
        finish_kernel,
        out_shape=(
            jax.ShapeDtypeStruct((owned, rank, feat), F32),
            jax.ShapeDtypeStruct((owned, rank, feat), F32),
            jax.ShapeDtypeStruct((owned, rank, bk.shape[2]), F32),
            jax.ShapeDtypeStruct((owned, rank, bk.shape[2]), F32),
        ),
        in_specs=[HBM],
        out_specs=(VMEM, VMEM, VMEM, VMEM),
        scratch_shapes=[pltpu.VMEM((owned, PART, LANE), F32), pltpu.SemaphoreType.DMA],
        compiler_params=PARAMS,
        name="finish",
    )(hbm(sums))
    return (grad_in, *grads)


def solution(mesh):
    n_dp, n_mp = mesh.devices.shape
    fine = Mesh(
        mesh.devices.reshape(n_dp // 2, 2, 4, n_mp // 8, 2), ("zh", "zl", "y", "x", "core")
    )
    dp, mp = ("zh", "zl"), ("y", "x", "core")
    rows = P((*dp, *mp), None)
    in_specs = (
        rows, rows, rows,
        P(mp, None), P(mp, None),
        P(None, None, mp), P(None, None, mp), P(None, None, mp), P(None, None, mp),
        P(dp, None), P(dp, None),
    )
    grads = P(dp, None, mp)
    return jax.shard_map(
        shards, mesh=fine, in_specs=in_specs, out_specs=(rows, grads, grads, grads, grads),
        check_vma=False,
    )
```
